32 devices in a mesh: dp: 4 (over z), fsdp: 8 (over y, x, core).
Axes of the slice: x: 2, y: 2, z: 4, core: 2. Of those that a mesh axis runs over, the one named last changes fastest.
Arguments:
- txt_tokens: bfloat16 [32, 8, 3072], P(('dp', 'fsdp')), may hold values from -6 to 6
- concept_table: bfloat16 [1024, 3072], P('dp'), may hold values from -6 to 6
- concept_ids: int32 [32], P(('dp', 'fsdp')), may hold values from 0 to 1023
- positions: int32 [32], P(('dp', 'fsdp')), may hold values from 0 to 7
- timesteps: int32 [32], P(('dp', 'fsdp')), may hold values from 0 to 63
- counts: int32 [1024], P('dp'), may hold values from 1 to 16
- mod_table: bfloat16 [64, 2, 3072], P(None, None, 'fsdp'), may hold values from -1.5 to 1.5
- kv_weight: bfloat16 [3072, 3072], P('fsdp'), may hold values from -0.109375 to 0.109375
- kv_bias: float32 [3072], replicated, may hold values from -3 to 3
- key_gain: float32 [128], replicated, may hold values from 0.5 to 1.5
- img_query: bfloat16 [32, 192, 1536], P(('dp', 'fsdp')), may hold values from -256 to 256
- img_key: bfloat16 [32, 192, 1536], P(('dp', 'fsdp')), may hold values from -6 to 6
- img_value: bfloat16 [32, 192, 1536], P(('dp', 'fsdp')), may hold values from -6 to 6
- out_grad: bfloat16 [32, 192, 1536], P(('dp', 'fsdp')), may hold values from -6 to 6
Outputs:
- table_grad: float32 [1024, 3072], P('dp', 'fsdp')
The draws below stay inside these ranges and needn't reach their ends.
Inputs may be any that keep to these rules, and one draw needn't show every extreme that they name: `concept_ids`: concept of each sample, some concepts far more common than others.
All inputs are finite; a program needn't handle non-finite values.
Results may differ from the reference program's by a relative error of at most 0.0083.
Values may be sent and summed in bfloat16 or wider, within the bound.
No kernel may reach another device: no remote copies, remote signals or barrier semaphores. Data moves between devices by JAX's collectives and lax.ppermute only.
A program may use at most 64 MiB of HBM per device.

```python
import math
import jax
import jax.numpy as jnp
import numpy as np
from jax import lax

D = 3072
HEADS = 12
DH = 128
HW = 1536
LT = 8
LI = 192
NT = 64
CONCEPTS = 1024
SAMPLES = 32


def draw_pair(key):
    shape = (SAMPLES, LI, HEADS * DH)
    keys_v = jnp.clip(jax.random.normal(jax.random.fold_in(key, 101), shape, jnp.float32), -6.0, 6.0)
    query_v = jnp.clip(jax.random.normal(jax.random.fold_in(key, 202), shape, jnp.float32), -6.0, 6.0)
    return (query_v, keys_v)


def draw_img_query(key, part):
    return draw_pair(key)[0].astype(jnp.bfloat16)


def draw_img_key(key, part):
    return draw_pair(key)[1].astype(jnp.bfloat16)


def with_ends(drawn, rng, smallest, high):
    dims = drawn.shape
    index_at = [jax.random.randint(jax.random.fold_in(rng, axis), (), 0, dims[axis]) for axis in range(len(dims))]
    drawn = drawn.at[tuple(index_at)].set(smallest)
    longest = dims.index(max(dims))
    index_at[longest] = (index_at[longest] + 1) % dims[longest]
    return drawn.at[tuple(index_at)].set(high)


def block_levels(stream_key, extent, split, low, largest):
    gain, own = 1.0, jax.random.fold_in(stream_key, 6)
    for axis_at, parts in split:
        draws = jnp.exp(jax.random.uniform(jax.random.fold_in(own, axis_at), (parts,), jnp.float32, low / len(split), largest / len(split)))
        gain = gain * jnp.repeat(draws, extent[axis_at] // parts).reshape([-1 if axis == axis_at else 1 for axis in range(len(extent))])
    return gain


def rank_bounds(amount, lean):
    portions = [(1 << 20) // math.isqrt(rank ** lean) + 1 for rank in range(1, amount + 1)]
    scale = 1 + sum(portions) // (1 << 30)
    return np.cumsum(np.array([max(1, weight // scale) for weight in portions]))


def skewed_ids(rng, dims, amount, skew):
    grid = rank_bounds(amount, skew)
    lot = jax.random.randint(jax.random.fold_in(rng, 1), dims, 0, int(grid[amount - 1]))
    grade = jnp.searchsorted(jnp.asarray(grid, jnp.int32), lot, side="right")
    return jax.random.permutation(jax.random.fold_in(rng, 2), amount)[grade].astype(jnp.int32)


def scatter_about(own_key, shape, width, limit, pieces=(), held_as=jnp.bfloat16):
    values = width * jax.random.normal(own_key, shape, jnp.float32)
    if pieces:
        values = values * block_levels(own_key, shape, pieces, -0.22, 0.18)
    return jnp.clip(values, -limit, limit).astype(held_as)


def setup_inputs(seed: int = 0) -> dict:
    splits = jax.random.split(jax.random.key(seed), 15)
    txt_tokens = scatter_about(splits[0], (SAMPLES, LT, D), 1.0, 6.0, ((0, 32),))
    concept_table = scatter_about(splits[1], (CONCEPTS, D), 1.0, 6.0, ((0, 4),))
    concept_ids = with_ends(skewed_ids(splits[2], (SAMPLES,), CONCEPTS, 2), jax.random.fold_in(splits[2], 3), 0, CONCEPTS - 1).astype(jnp.int32)
    positions = with_ends(jax.random.randint(splits[3], (SAMPLES,), 0, LT), jax.random.fold_in(splits[3], 1), 0, LT - 1).astype(jnp.int32)
    timesteps = with_ends(jax.random.randint(splits[4], (SAMPLES,), 0, NT), jax.random.fold_in(splits[4], 1), 0, NT - 1).astype(jnp.int32)
    counts = with_ends(jax.random.randint(splits[5], (CONCEPTS,), 1, 17), jax.random.fold_in(splits[5], 1), 1, 16).astype(jnp.int32)
    mod_table = scatter_about(splits[6], (NT, 2, D), 0.3, 1.5, ((2, 8),))
    kv_weight = scatter_about(splits[7], (D, 2 * HW), D ** -0.5, 0.109375, ((0, 8),))
    kv_bias = scatter_about(splits[8], (2 * HW,), 0.5, 3.0, (), jnp.float32)
    key_gain = jnp.clip(1.0 + 0.1 * jax.random.normal(splits[9], (DH,), jnp.float32), 0.5, 1.5)
    img_query = draw_img_query(jax.random.fold_in(splits[14], 71), 0)
    img_key = draw_img_key(jax.random.fold_in(splits[14], 71), 0)
    img_value = scatter_about(splits[12], (SAMPLES, LI, HW), 1.0, 6.0, ((0, 32),))
    out_grad = scatter_about(splits[13], (SAMPLES, LI, HW), 1.0, 6.0, ((0, 32),))
    return dict(txt_tokens=txt_tokens, concept_table=concept_table, concept_ids=concept_ids, positions=positions, timesteps=timesteps, counts=counts, mod_table=mod_table, kv_weight=kv_weight, kv_bias=kv_bias, key_gain=key_gain, img_query=img_query, img_key=img_key, img_value=img_value, out_grad=out_grad)


EPSILON = 1e-06

def layer_norm(values):
    centre = lax.optimization_barrier(jnp.mean(values, -1, keepdims=True))
    spread = lax.optimization_barrier(jnp.mean((values - centre) ** 2, -1, keepdims=True))
    inverse = lax.rsqrt(spread + EPSILON)
    return ((values - centre) * inverse, inverse[..., 0])

def reference(txt_tokens, concept_table, concept_ids, positions, timesteps, counts, mod_table, kv_weight, kv_bias, key_gain, img_query, img_key, img_value, out_grad):
    table_hat, table_rstd = layer_norm(concept_table.astype(jnp.float32))
    table_hat = table_hat.astype(jnp.bfloat16)
    weight_f = kv_weight.astype(jnp.float32)
    root_dh = jnp.sqrt(jnp.float32(DH))

    def one_sample(packed):
        tokens, concept, place, bucket, queries, img_keys, img_vals, grad_out = packed
        own_hat = layer_norm(tokens.astype(jnp.float32))[0].astype(jnp.bfloat16)
        concept_row = lax.dynamic_index_in_dim(table_hat, concept, 0, keepdims=False)
        is_place = (jnp.arange(LT, dtype=jnp.int32) == place)[:, None]
        normed = jnp.where(is_place, concept_row[None, :], own_hat)
        modul = lax.dynamic_index_in_dim(mod_table, bucket, 0, keepdims=False).astype(jnp.float32)
        shift_row = modul[0]
        scale_row = 1.0 + modul[1]
        modulated = (scale_row * normed.astype(jnp.float32) + shift_row).astype(jnp.bfloat16)
        kv_rows = jnp.dot(modulated, kv_weight, preferred_element_type=jnp.float32) + kv_bias
        key_raw = kv_rows[:, :HW].reshape(LT, HEADS, DH)
        key_inv = lax.rsqrt(lax.optimization_barrier(jnp.mean(key_raw * key_raw, -1)) + EPSILON)
        key_norm = (key_raw * key_inv[..., None] * key_gain).astype(jnp.bfloat16).reshape(LT, HW)
        val_txt = kv_rows[:, HW:].astype(jnp.bfloat16)
        keys_all = jnp.concatenate([key_norm, img_keys], 0).astype(jnp.float32).reshape(LT + LI, HEADS, DH)
        vals_all = jnp.concatenate([val_txt, img_vals], 0).astype(jnp.float32).reshape(LT + LI, HEADS, DH)
        query_f = queries.astype(jnp.float32).reshape(LI, HEADS, DH)
        scores = jnp.einsum('qhd,khd->hqk', query_f, keys_all) / root_dh
        row_top = lax.optimization_barrier(jnp.max(scores, -1, keepdims=True))
        raised = jnp.exp(scores - row_top)
        prob_full = raised / lax.optimization_barrier(jnp.sum(raised, -1, keepdims=True))
        prob_low = lax.optimization_barrier(prob_full.astype(jnp.bfloat16))
        attended = jnp.einsum('hqk,khd->qhd', prob_low.astype(jnp.float32), vals_all)
        grad_f = grad_out.astype(jnp.float32).reshape(LI, HEADS, DH)
        row_delta = jnp.einsum('qhd,qhd->hq', grad_f, attended)
        prob_pos = lax.dynamic_index_in_dim(prob_full, place, 2, keepdims=False)
        val_pos = lax.dynamic_index_in_dim(vals_all, place, 0, keepdims=False)
        grad_prob = jnp.einsum('qhd,hd->hq', grad_f, val_pos)
        grad_score = prob_pos * (grad_prob - row_delta)
        grad_val = jnp.einsum('hq,qhd->hd', prob_pos, grad_f)
        grad_key = jnp.einsum('hq,qhd->hd', grad_score, query_f) / root_dh
        raw_pos = lax.dynamic_index_in_dim(key_raw, place, 0, keepdims=False)
        inv_pos = lax.dynamic_index_in_dim(key_inv, place, 0, keepdims=False)
        normed_key = raw_pos * inv_pos[:, None]
        grad_norm = grad_key * key_gain
        grad_raw = inv_pos[:, None] * (grad_norm - normed_key * lax.optimization_barrier(jnp.mean(grad_norm * normed_key, -1, keepdims=True)))
        grad_kv = jnp.concatenate([grad_raw.reshape(HW), grad_val.reshape(HW)])
        grad_mod = jnp.dot(weight_f, grad_kv, precision=lax.Precision.HIGHEST) * scale_row
        concept_f = concept_row.astype(jnp.float32)
        return grad_mod - jnp.mean(grad_mod) - concept_f * jnp.mean(grad_mod * concept_f)
    row_grad = lax.map(one_sample, (txt_tokens, concept_ids, positions, timesteps, img_query, img_key, img_value, out_grad))
    summed = jax.ops.segment_sum(row_grad, concept_ids, num_segments=CONCEPTS)
    return summed * (table_rstd / counts.astype(jnp.float32))[:, None]
```

```python
import functools
import math

import jax
import jax.numpy as jnp
import numpy as np
from jax import lax
from jax.experimental import pallas as pl
from jax.experimental.pallas import tpu as pltpu
from jax.sharding import Mesh, PartitionSpec as P

EPSILON = 1e-06
BF16 = jnp.bfloat16
F32 = jnp.float32
VMEM_BYTES = 63 * 1024 * 1024 + 512 * 1024
NT = (((1,), (1,)), ((), ()))


def dot(a, b):
    return jnp.dot(a, b, preferred_element_type=F32)


def dot_nt(a, b):
    return lax.dot_general(a, b, NT, preferred_element_type=F32)


def split_bf16(x):
    high = x.astype(BF16)
    return high, (x - high.astype(F32)).astype(BF16)


def whole(*shape):
    return pl.BlockSpec(shape, lambda *_: (0,) * len(shape))


def params(**kw):
    return pltpu.CompilerParams(vmem_limit_bytes=VMEM_BYTES, **kw)


def token_norm_kernel(x_ref, out_ref):
    x = x_ref[...].astype(F32)
    d = x - jnp.mean(x, -1, keepdims=True)
    out_ref[...] = (d * lax.rsqrt(jnp.mean(d * d, -1, keepdims=True) + EPSILON)).astype(BF16)


def token_norm(tokens):
    return pl.pallas_call(
        token_norm_kernel, out_shape=jax.ShapeDtypeStruct(tokens.shape, BF16), compiler_params=params()
    )(tokens)


def table_norm_kernel(n_parts, x_ref, *refs):
    parts, hats, rstd_ref = refs[:n_parts], refs[n_parts : 2 * n_parts], refs[-1]
    x = x_ref[...].astype(F32)
    mean = jnp.mean(x, -1, keepdims=True)
    d = x - mean
    rstd = lax.rsqrt(jnp.mean(d * d, -1, keepdims=True) + EPSILON)
    rstd_ref[...] = rstd
    for part, hat in zip(parts, hats):
        hat[...] = ((part[...].astype(F32) - mean) * rstd).astype(BF16)


def table_norm(table, parts):
    rows, width = table.shape
    block = math.gcd(rows, 64)
    row_spec = lambda w: pl.BlockSpec((block, w), lambda i: (i, 0))
    widths = [p.shape[1] for p in parts]
    out = pl.pallas_call(
        functools.partial(table_norm_kernel, len(parts)),
        grid=(rows // block,),
        in_specs=[row_spec(width)] + [row_spec(w) for w in widths],
        out_specs=[row_spec(w) for w in widths] + [row_spec(1)],
        out_shape=[jax.ShapeDtypeStruct((rows, w), BF16) for w in widths]
        + [jax.ShapeDtypeStruct((rows, 1), F32)],
        compiler_params=params(),
    )(table, *parts)
    return out[:-1], out[-1]


def image_kernel(head_dim, q_ref, k_ref, v_ref, g_ref, out_ref):
    scale = 1.0 / math.sqrt(head_dim)
    for h in range(q_ref.shape[1] // head_dim):
        cols = slice(h * head_dim, (h + 1) * head_dim)
        s = dot_nt(k_ref[:, cols], q_ref[:, cols]) * scale
        gv = dot_nt(v_ref[:, cols], g_ref[:, cols])
        top = jnp.max(s, 0, keepdims=True)
        e = jnp.exp(s - top)
        out_ref[h, 0:1, :] = top
        out_ref[h, 1:2, :] = jnp.sum(e, 0, keepdims=True)
        out_ref[h, 2:3, :] = jnp.sum(e * gv, 0, keepdims=True)


def image_part(q, k, v, g, head_dim):
    rows, width = q.shape
    heads = width // head_dim
    per = math.gcd(heads, 3)
    spec = pl.BlockSpec((rows, per * head_dim), lambda i: (0, i))
    return pl.pallas_call(
        functools.partial(image_kernel, head_dim),
        grid=(heads // per,),
        in_specs=[spec] * 4,
        out_specs=pl.BlockSpec((per, 8, rows), lambda i: (i, 0, 0)),
        out_shape=jax.ShapeDtypeStruct((heads, 8, rows), F32),
        compiler_params=params(),
    )(q, k, v, g)


def project_kernel(dims, here_ref, labels_ref, *refs):
    n_dp, n_chip, n_core, tok_len, conc_dev, buckets, col_block, head_dim = dims
    mods, hats = refs[:n_core], refs[n_core : 2 * n_core]
    toks = refs[2 * n_core : 2 * n_core + n_chip]
    weights = refs[2 * n_core + n_chip : 3 * n_core + n_chip]
    rest = refs[3 * n_core + n_chip :]
    conc_out, tok_outs, lhs = rest[0], rest[1 : 1 + n_chip], rest[1 + n_chip]
    n_all = n_dp * n_chip
    n_tok = n_chip * tok_len

    @pl.when(pl.program_id(0) == 0)
    def _():
        my_dp, my_chip, my_core = here_ref[0], here_ref[1], here_ref[2]
        labels = labels_ref[:, 0, :].reshape(n_all, n_core, labels_ref.shape[2])
        mine = jnp.where(lax.broadcasted_iota(jnp.int32, labels.shape, 1) == my_core, labels, 0)
        mine = jnp.sum(mine, 1)
        ids, times = mine[:, 0:1], mine[:, 2:3]
        lanes = lambda r, n: lax.broadcasted_iota(jnp.int32, (r, n), 1)
        pick_time = (lanes(n_all, buckets) == times).astype(BF16)
        pick_row = (lanes(n_all, conc_dev) == ids - my_dp * conc_dev).astype(BF16)

        def owned_by(step):
            first = lax.rem(my_dp + n_dp - step, n_dp) * conc_dev
            return (ids >= first) & (ids < first + conc_dev)

        tok_times = jnp.concatenate(
            [
                jnp.broadcast_to(
                    labels_ref[(my_dp * n_chip + (my_chip ^ s)) * n_core + my_core][:, 2:3],
                    (tok_len, 1),
                )
                for s in range(n_chip)
            ],
            0,
        )
        pick_tok = (lanes(n_tok, buckets) == tok_times).astype(BF16)
        for p in range(n_core):
            shift, scale = mods[p][0], mods[p][1]
            scale_c, shift_c = 1.0 + dot(pick_time, scale), dot(pick_time, shift)
            conc = scale_c * dot(pick_row, hats[p][...]) + shift_c
            conc = conc.astype(BF16).astype(F32)
            rows = jnp.where(
                owned_by(0),
                conc,
                jnp.where(owned_by(1), scale_c, jnp.where(owned_by(2), shift_c, 0.0)),
            )
            high, low = split_bf16(rows)
            tok = jnp.concatenate([t[p].astype(F32) for t in toks], 0)
            tok = (1.0 + dot(pick_tok, scale)) * tok + dot(pick_tok, shift)
            lhs[p, 0:n_tok] = tok.astype(BF16)
            lhs[p, n_tok : n_tok + n_all] = high
            lhs[p, n_tok + n_all : n_tok + 2 * n_all] = low

    out = dot(lhs[0], weights[0][...])
    for p in range(1, n_core):
        out += dot(lhs[p], weights[p][...])
    conc = out[n_tok : n_tok + n_all] + out[n_tok + n_all :]
    for r in range(col_block // head_dim):
        conc_out[:, r, :] = conc[:, r * head_dim : (r + 1) * head_dim]
    for s in range(n_chip):
        tok_outs[s][...] = out[s * tok_len : (s + 1) * tok_len].astype(BF16)


def project(here, labels, mods, hats, toks, weights, sizes, head_dim):
    n_dp, n_chip, n_core = sizes
    tok_len = toks[0].shape[1]
    width, kv_width = weights[0].shape
    conc_dev, buckets = hats[0].shape[0], mods[0].shape[1]
    col_block = 8 * head_dim
    n_all, n_tok = n_dp * n_chip, n_chip * tok_len
    dims = (n_dp, n_chip, n_core, tok_len, conc_dev, buckets, col_block, head_dim)
    out = pl.pallas_call(
        functools.partial(project_kernel, dims),
        grid=(kv_width // col_block,),
        in_specs=[pl.BlockSpec(memory_space=pltpu.SMEM), whole(*labels.shape)]
        + [whole(*m.shape) for m in mods]
        + [whole(*h.shape) for h in hats]
        + [whole(*t.shape) for t in toks]
        + [pl.BlockSpec((width, col_block), lambda i: (0, i))] * n_core,
        out_specs=[pl.BlockSpec((n_all, 8, head_dim), lambda i: (0, i, 0))]
        + [pl.BlockSpec((tok_len, col_block), lambda i: (0, i))] * n_chip,
        out_shape=[jax.ShapeDtypeStruct((n_all, kv_width // head_dim, head_dim), F32)]
        + [jax.ShapeDtypeStruct((tok_len, kv_width), BF16)] * n_chip,
        scratch_shapes=[pltpu.VMEM((n_core, n_tok + 2 * n_all, width), BF16)],
        compiler_params=params(),
    )(here, labels, *mods, *hats, *toks, *weights)
    return out[0], out[1:]


def sample_kernel(dims, place_ref, conc_ref, bias_ref, gain_ref, stat_ref, q_ref, g_ref, *refs):
    n_chip, head_dim, model_width, n_dev = dims
    toks, out_ref = refs[:n_chip], refs[n_chip]
    heads = stat_ref.shape[0]
    scale = 1.0 / math.sqrt(head_dim)
    tok_len = toks[0].shape[0]
    kv = toks[0][...].astype(F32)
    for t in toks[1:]:
        kv += t[...].astype(F32)

    def gathered(i):
        total = conc_ref[place_ref[i] * n_chip]
        for s in range(1, n_chip):
            total += conc_ref[place_ref[i] * n_chip + s]
        return total

    conc, scale_sum, shift_sum = gathered(0), gathered(1), gathered(2)
    at_pos = lax.broadcasted_iota(jnp.int32, (tok_len, 1), 0) == place_ref[3]
    row = lax.broadcasted_iota(jnp.int32, (8, 1), 0)
    gain = gain_ref[...]
    rows = []
    for i in range(2 * heads):
        cols = slice(i * head_dim, (i + 1) * head_dim)
        rows.append(jnp.where(at_pos, conc[i : i + 1, :], kv[:, cols]) + bias_ref[:, cols])

    def pick(x):
        return jnp.sum(jnp.where(at_pos, x, 0.0), 0, keepdims=True)

    def contract(weights, cols, ref):
        high, low = split_bf16(weights)
        both = jnp.where(row == 0, high.astype(F32), jnp.where(row == 1, low.astype(F32), 0.0))
        return jnp.sum(dot(both.astype(BF16), ref[:, cols]), 0, keepdims=True)

    raw_rows, val_rows = [], []
    for h in range(heads):
        cols = slice(h * head_dim, (h + 1) * head_dim)
        raw = rows[h]
        inv = lax.rsqrt(jnp.mean(raw * raw, -1, keepdims=True) + EPSILON)
        key = (raw * inv * gain).astype(BF16)
        val = rows[heads + h].astype(BF16)
        s = dot_nt(key, q_ref[:, cols]) * scale
        gv = dot_nt(val, g_ref[:, cols])
        top, total, weighted = stat_ref[h, 0:1, :], stat_ref[h, 1:2, :], stat_ref[h, 2:3, :]
        new_top = jnp.maximum(top, jnp.max(s, 0, keepdims=True))
        e = jnp.exp(s - new_top)
        keep = jnp.exp(top - new_top)
        inv_total = 1.0 / (total * keep + jnp.sum(e, 0, keepdims=True))
        delta = (weighted * keep + jnp.sum(e * gv, 0, keepdims=True)) * inv_total
        p = pick(e) * inv_total
        dscore = p * (pick(gv) - delta)
        val_rows.append(contract(p, cols, g_ref))
        dkey = contract(dscore, cols, q_ref) * scale
        inv_pos = pick(inv)
        normed = pick(raw) * inv_pos
        dn = dkey * gain
        raw_rows.append(inv_pos * (dn - normed * jnp.mean(dn * normed, -1, keepdims=True)))
    dkv = jnp.concatenate(raw_rows + val_rows, 0)

    def total_of(x):
        return jnp.sum(jnp.sum(x, 0, keepdims=True), 1, keepdims=True) * (1.0 / model_width)

    mean_1 = split_bf16(total_of(dkv * scale_sum))
    mean_2 = split_bf16(total_of(dkv * (conc - shift_sum)))
    lane = lax.broadcasted_iota(jnp.int32, (8, head_dim), 1)
    side = jnp.zeros((8, head_dim), F32)
    for i, x in enumerate(mean_1 + mean_2):
        side = jnp.where(lane == i, x.astype(F32), side)
    packet = jnp.concatenate([dkv, side], 0).astype(BF16)
    out_ref[...] = jnp.broadcast_to(packet[None], out_ref.shape)


def sample_part(place, conc, bias, gain, stats, q, g, toks, n_dev, model_width):
    n_chip, head_dim = len(toks), gain.shape[1]
    rows = conc.shape[1] + 8
    vmem = pl.BlockSpec(memory_space=pltpu.VMEM)
    return pl.pallas_call(
        functools.partial(sample_kernel, (n_chip, head_dim, model_width, n_dev)),
        in_specs=[pl.BlockSpec(memory_space=pltpu.SMEM)] + [vmem] * (6 + n_chip),
        out_specs=vmem,
        out_shape=jax.ShapeDtypeStruct((n_dev, rows, head_dim), BF16),
        compiler_params=params(),
    )(place, conc, bias, gain, stats, q, g, *toks)


def owner_kernel(dims, here_ref, packet_ref, labels_ref, ids_ref, mod_ref, hat_ref, coef_ref, w_ref, out_ref, flat):
    conc_dev, buckets = dims
    n_dev, rows, head_dim = packet_ref.shape
    parts = w_ref.shape[1] // head_dim
    first = here_ref[0] * conc_dev
    flat[...] = packet_ref[...].reshape(n_dev * rows, head_dim).astype(F32)
    piece = lambda r: flat[pl.ds(r, n_dev, stride=rows), :]
    dkv = jnp.concatenate([piece(r).astype(BF16) for r in range(parts)], 1)
    side = piece(parts)
    mean_1 = side[:, 0:1] + side[:, 1:2]
    mean_2 = side[:, 2:3] + side[:, 3:4]
    labels = labels_ref[:, 0, :]
    ids, times = labels[:, 0:1], labels[:, 2:3]
    lanes = lambda n: lax.broadcasted_iota(jnp.int32, (n_dev, n), 1)
    scale = 1.0 + dot((lanes(buckets) == times).astype(BF16), mod_ref[1])
    conc = dot((lanes(conc_dev) == ids - first).astype(BF16), hat_ref[...])
    grad = dot_nt(dkv, w_ref[...]) * scale - mean_1 - conc * mean_2
    high, low = split_bf16(grad)
    one_hot = lax.broadcasted_iota(jnp.int32, (conc_dev, n_dev), 0) == ids_ref[...] - first
    one_hot = one_hot.astype(BF16)
    out_ref[...] = (dot(one_hot, high) + dot(one_hot, low)) * coef_ref[...]


def owner_part(here, packets, labels, ids, mod, hat, coef, weight):
    conc_dev, width = hat.shape
    n_dev, rows, head_dim = packets.shape
    vmem = pl.BlockSpec(memory_space=pltpu.VMEM)
    return pl.pallas_call(
        functools.partial(owner_kernel, (conc_dev, mod.shape[1])),
        in_specs=[pl.BlockSpec(memory_space=pltpu.SMEM)] + [vmem] * 7,
        out_specs=vmem,
        out_shape=jax.ShapeDtypeStruct((conc_dev, width), F32),
        scratch_shapes=[pltpu.VMEM((n_dev * rows, head_dim), F32)],
        compiler_params=params(),
    )(here, packets, labels, ids, mod, hat, coef, weight)


def shards(
    txt_tokens,
    concept_table,
    concept_ids,
    positions,
    timesteps,
    counts,
    mod_table,
    kv_weight,
    kv_bias,
    key_gain,
    img_query,
    img_key,
    img_value,
    out_grad,
):
    everyone = ("dp", "chip", "core")
    n_dp, n_chip, n_core = (lax.axis_size(a) for a in everyone)
    n_dev = n_dp * n_chip * n_core
    my_dp, my_chip, my_core = (lax.axis_index(a) for a in everyone)
    model_width = txt_tokens.shape[2]
    slice_width = kv_weight.shape[0]
    head_dim = key_gain.shape[0]
    conc_dev = concept_table.shape[0]
    here = jnp.stack([my_dp, my_chip, my_core]).astype(jnp.int32)

    labels = jnp.stack([concept_ids[0], positions[0], timesteps[0]])
    labels = jnp.pad(labels, (0, 125))
    labels = lax.all_to_all(
        jnp.broadcast_to(labels[None, None, :], (n_dev, 1, 128)), everyone, 0, 0, tiled=True
    )

    def from_core(x, s):
        return x if s == 0 else lax.ppermute(x, "core", [(i, i ^ s) for i in range(n_core)])

    def from_chip(x, s):
        return x if s == 0 else lax.ppermute(x, "chip", [(i, i ^ s) for i in range(n_chip)])

    def feature_slice(x, chip, s):
        part = chip * n_core + (my_core ^ s)
        return lax.dynamic_slice_in_dim(x, part * slice_width, slice_width, 1)

    own_hat = token_norm(txt_tokens[0])
    toks = [
        from_chip(
            jnp.stack([feature_slice(own_hat, my_chip ^ s, p) for p in range(n_core)]), s
        )
        for s in range(n_chip)
    ]
    weights = [from_core(kv_weight, s) for s in range(n_core)]
    mod_own = jnp.transpose(mod_table, (1, 0, 2))
    mods = [from_core(mod_own, s) for s in range(n_core)]
    hats, rstd = table_norm(
        concept_table, [feature_slice(concept_table, my_chip, s) for s in range(n_core)]
    )
    coef = rstd / counts.astype(F32)[:, None]
    stats = image_part(img_query[0], img_key[0], img_value[0], out_grad[0], head_dim)

    conc, tok_terms = project(
        here, labels, mods, hats, toks, weights, (n_dp, n_chip, n_core), head_dim
    )
    tok_rows = [from_chip(t, s) for s, t in enumerate(tok_terms)]
    conc = lax.all_to_all(conc, ("dp", "chip"), 0, 0, tiled=True)

    owner = concept_ids[0] // conc_dev
    place = jnp.stack([owner, (owner + 1) % n_dp, (owner + 2) % n_dp, positions[0]])
    packets = sample_part(
        place, conc, kv_bias[None], key_gain[None], stats, img_query[0], out_grad[0],
        tok_rows, n_dev, model_width,
    )
    packets = lax.all_to_all(packets, everyone, 0, 0, tiled=True)
    ids = labels[:, 0, 0][None, :]
    return owner_part(here, packets, labels, ids, mod_own, hats[0], coef, kv_weight)


def solution(mesh):
    n_dp, n_fsdp = mesh.shape["dp"], mesh.shape["fsdp"]
    n_core = 2 if n_fsdp % 2 == 0 else 1
    fine = Mesh(mesh.devices.reshape(n_dp, n_fsdp // n_core, n_core), ("dp", "chip", "core"))
    fsdp = ("chip", "core")
    every = ("dp",) + fsdp
    placed = (
        P(every, None, None),
        P("dp", None),
        P(every),
        P(every),
        P(every),
        P("dp"),
        P(None, None, fsdp),
        P(fsdp, None),
        P(),
        P(),
        P(every, None, None),
        P(every, None, None),
        P(every, None, None),
        P(every, None, None),
    )
    return jax.shard_map(
        shards, mesh=fine, in_specs=placed, out_specs=P("dp", fsdp), check_vma=False
    )
```

```python
import functools
import math

import jax
import jax.numpy as jnp
from jax import lax
from jax.experimental import pallas as pl
from jax.experimental.pallas import tpu as pltpu
from jax.sharding import Mesh, PartitionSpec as P

EPSILON = 1e-06
BF16 = jnp.bfloat16
F32 = jnp.float32
I32 = jnp.int32
LANES = 128
MIB = 1024 * 1024
NT = (((1,), (1,)), ((), ()))
TN = (((0,), (0,)), ((), ()))
EVERYONE = ("dp", "chip", "core")
CLASS = ("dp", "chip")


def dot(a, b):
    return jnp.dot(a, b, preferred_element_type=F32)


def dot_nt(a, b):
    return lax.dot_general(a, b, NT, preferred_element_type=F32)


def dot_tn(a, b):
    return lax.dot_general(a, b, TN, preferred_element_type=F32)


def split_bf16(x):
    high = x.astype(BF16)
    return high, (x - high.astype(F32)).astype(BF16)


def iota(shape, axis):
    return lax.broadcasted_iota(I32, shape, axis)


def hold(x):
    return ("hold", x)


def late(x, chunks, axis=1):
    return ("late", x, chunks, axis)


def scalar(x):
    return ("scalar", x)


def call(body, operands, results, scratch=(), vmem=62, flops=2_000_000_000):
    arrays = [o[1] for o in operands]
    shapes = [jax.ShapeDtypeStruct(*r) for r in results]
    n_in, n_out = len(arrays), len(shapes)
    counts = [o[2] if o[0] == "late" else 1 for o in operands]
    offsets = [sum(counts[:i]) for i in range(n_in)]
    n_sems = sum(counts) + n_out

    def kernel(*refs):
        ins, outs = refs[:n_in], refs[n_in : n_in + n_out]
        held, made = refs[n_in + n_out : 2 * n_in + n_out], refs[2 * n_in + n_out : 2 * n_in + 2 * n_out]
        sems, extra = refs[2 * (n_in + n_out)], refs[2 * (n_in + n_out) + 1 :]

        def copies_of(i):
            o = operands[i]
            if o[0] != "late" or o[2] == 1:
                return [pltpu.make_async_copy(ins[i], held[i], sems.at[offsets[i]])]
            size = o[1].shape[o[3]] // o[2]
            cut = lambda k: tuple([slice(None)] * o[3] + [pl.ds(k * size, size)])
            return [
                pltpu.make_async_copy(ins[i].at[cut(k)], held[i].at[cut(k)], sems.at[offsets[i] + k])
                for k in range(o[2])
            ]

        copies = [copies_of(i) for i in range(n_in)]
        first = [c for i in range(n_in) if operands[i][0] != "late" for c in copies[i]]
        then = [i for i in range(n_in) if operands[i][0] == "late"]
        for c in first:
            c.start()
        for k in range(max([counts[i] for i in then], default=0)):
            for i in then:
                if k < counts[i]:
                    copies[i][k].start()
        for c in first:
            c.wait()
        given = [
            (held[i], lambda k, i=i: copies[i][k].wait()) if operands[i][0] == "late" else held[i]
            for i in range(n_in)
        ]
        body(given, made, extra)
        final = [
            pltpu.make_async_copy(m, out, sems.at[sum(counts) + k])
            for k, (m, out) in enumerate(zip(made, outs))
        ]
        for c in final:
            c.start()
        for c in final:
            c.wait()

    place = lambda o: pltpu.SMEM if o[0] == "scalar" else pltpu.VMEM
    return pl.pallas_call(
        kernel,
        in_specs=[pl.BlockSpec(memory_space=pltpu.HBM)] * n_in,
        out_specs=[pl.BlockSpec(memory_space=pltpu.HBM)] * n_out,
        out_shape=shapes,
        scratch_shapes=[place(o)(o[1].shape, o[1].dtype) for o in operands]
        + [pltpu.VMEM(s.shape, s.dtype) for s in shapes]
        + [pltpu.SemaphoreType.DMA((n_sems,))]
        + list(scratch),
        compiler_params=pltpu.CompilerParams(vmem_limit_bytes=vmem * MIB),
        cost_estimate=pl.CostEstimate(flops=flops, bytes_accessed=1024, transcendentals=0),
    )(*arrays)


def normalise(x):
    d = x - jnp.mean(x, -1, keepdims=True)
    rstd = lax.rsqrt(jnp.mean(d * d, -1, keepdims=True) + EPSILON)
    return d * rstd, rstd


def tokens_per_dp(sizes, tok_len):
    return -(-tok_len // sizes[0])


def packet_rows(per, n_core, width):
    need = -(-per * n_core * width // LANES) + 1
    return need, -(-need // 16) * 16


def pack_body(sizes, width, per, ins, outs, scratch):
    n_dp, n_chip, n_core = sizes
    ids, places, times, tokens = ins
    (out,), (held, flat) = outs, scratch
    tok_len = tokens.shape[0]
    need, rows = packet_rows(per, n_core, width)
    pieces = width // LANES
    held[...] = normalise(tokens[...].astype(F32))[0]
    flat[...] = jnp.zeros(flat.shape, F32)
    lane = iota((1, LANES), 1)
    values = (ids[0] // 64, lax.rem(ids[0], 64), places[0], times[0])
    label = jnp.zeros((1, LANES), F32)
    for i, x in enumerate(values):
        label = jnp.where(lane == i, x.astype(F32), label)
    core = lax.axis_index("core")
    for d in range(n_dp):
        for chip in range(n_chip):
            base = (d * n_chip + chip) * rows
            flat[base + need - 1 : base + need, :] = label
            for i in range(per):
                t = d * per + i
                for p in range(n_core if t < tok_len else 0):
                    at = (chip * n_core + (core ^ p)) * width
                    for k in range(pieces):
                        r = base + (i * n_core + p) * pieces + k
                        lanes = pl.ds(pl.multiple_of(at + k * LANES, LANES), LANES)
                        flat[r : r + 1, :] = held[t : t + 1, lanes]
    out[...] = flat[...].reshape(out.shape).astype(BF16)


def hat_body(ins, outs, scratch):
    outs[0][...] = normalise(ins[0][...].astype(F32))[0].astype(BF16)


def pack(ids, places, times, tokens, sizes, width):
    n_dp, n_chip, n_core = sizes
    n_all = n_dp * n_chip
    tok_len, model_width = tokens.shape
    per = tokens_per_dp(sizes, tok_len)
    need, rows = packet_rows(per, n_core, width)
    if width % LANES == 0:
        (out,) = call(
            functools.partial(pack_body, sizes, width, per),
            [scalar(ids), scalar(places), scalar(times), hold(tokens)],
            [((n_all, rows, LANES), BF16)],
            [pltpu.VMEM(tokens.shape, F32), pltpu.VMEM((n_all * rows, LANES), F32)],
        )
        return out
    (hat,) = call(hat_body, [hold(tokens)], [(tokens.shape, BF16)])
    hat = jnp.pad(hat, ((0, n_dp * per - tok_len), (0, 0)))
    hat = hat.reshape(n_dp, per, n_chip, n_core, width)
    core = lax.axis_index("core")
    own = [lax.dynamic_index_in_dim(hat, core ^ p, 3, keepdims=False) for p in range(n_core)]
    body = jnp.stack(own, 3).transpose(0, 2, 1, 3, 4).reshape(n_all, -1)
    body = jnp.pad(body, ((0, 0), (0, (need - 1) * LANES - body.shape[1])))
    label = jnp.stack([ids[0] // 64, ids[0] % 64, places[0], times[0]]).astype(BF16)
    label = jnp.broadcast_to(jnp.pad(label, (0, LANES - 4))[None], (n_all, LANES))
    out = jnp.concatenate([body, label], 1).reshape(n_all, need, LANES)
    return jnp.pad(out, ((0, 0), (0, rows - need), (0, 0)))


def table_body(width, n_core, ins, outs, scratch):
    (table, wait), mods, parts = ins[0], ins[1 : 1 + n_core], ins[1 + n_core :]
    hats, rstd_out, mod_outs = outs[:n_core], outs[n_core], outs[n_core + 1 :]
    chip, core = lax.axis_index("chip"), lax.axis_index("core")
    for mod, out in zip(mods, mod_outs):
        x = mod[...].astype(F32)
        out[0] = x[:, 0, :].astype(BF16)
        out[1] = x[:, 1, :].astype(BF16)
    rows = table.shape[0]
    block = rows // 4
    for i in range(4):
        wait(i)
        here = slice(i * block, (i + 1) * block)
        x = table[here, :].astype(F32)
        mean = jnp.mean(x, -1, keepdims=True)
        d = x - mean
        rstd = lax.rsqrt(jnp.mean(d * d, -1, keepdims=True) + EPSILON)
        rstd_out[here, :] = rstd
        for p in range(n_core):
            if parts:
                piece = parts[p][here, :]
            else:
                at = pl.multiple_of((chip * n_core + (core ^ p)) * width, LANES)
                piece = table[here, pl.ds(at, width)]
            hats[p][here, :] = ((piece.astype(F32) - mean) * rstd).astype(BF16)


def table_part(table, mods, width, n_core):
    rows = table.shape[0]
    buckets = mods[0].shape[0]
    parts = []
    if width % LANES:
        chip, core = lax.axis_index("chip"), lax.axis_index("core")
        cut = lambda p: lax.dynamic_slice_in_dim(table, (chip * n_core + (core ^ p)) * width, width, 1)
        parts = [hold(cut(p)) for p in range(n_core)]
    out = call(
        functools.partial(table_body, width, n_core),
        [late(table, 4, 0)] + [hold(m) for m in mods] + parts,
        [((rows, width), BF16)] * n_core + [((rows, 1), F32)] + [((2, buckets, width), BF16)] * n_core,
    )
    return out[:n_core], out[n_core], out[n_core + 1 :]


def image_body(head_dim, chunks, ins, outs, scratch):
    (q, _), (k, _), (v, _), (g, _) = ins
    (out,) = outs
    scale = 1.0 / math.sqrt(head_dim)
    heads = out.shape[0]
    for h in range(heads):
        if h % (heads // chunks) == 0:
            for _, wait in ins:
                wait(h // (heads // chunks))
        cols = slice(h * head_dim, (h + 1) * head_dim)
        s = dot_nt(k[:, cols], q[:, cols]) * scale
        gv = dot_nt(v[:, cols], g[:, cols])
        top = jnp.max(s, 0, keepdims=True)
        e = jnp.exp(s - top)
        out[h, 0:1, :] = top
        out[h, 1:2, :] = jnp.sum(e, 0, keepdims=True)
        out[h, 2:3, :] = jnp.sum(e * gv, 0, keepdims=True)


def image_part(q, k, v, g, head_dim):
    rows, width = q.shape
    heads = width // head_dim
    chunks = math.gcd(heads, 4)
    (out,) = call(
        functools.partial(image_body, head_dim, chunks),
        [late(x, chunks) for x in (q, k, v, g)],
        [((heads, 8, rows), F32)],
    )
    return out


def project_body(sizes, conc_dev, head_dim, per, chunks, ins, outs, scratch):
    n_dp, n_chip, n_core = sizes
    n_all = n_dp * n_chip
    mods, hats = ins[:n_core], ins[n_core : 2 * n_core]
    weights = ins[2 * n_core : 3 * n_core]
    given = ins[3 * n_core :]
    (out,), (lhs, flat, flat_in) = outs, scratch
    width, kv_width = weights[0][0].shape
    buckets = mods[0].shape[1]
    my_dp = lax.axis_index("dp")
    if len(given) == 1:
        need, rows = packet_rows(per, n_core, width)
        pieces = width // LANES
        flat_in[...] = given[0][...].reshape(n_all * rows, LANES).astype(F32)
        row = lambda r: flat_in[pl.ds(r, n_all, stride=rows), :]
        labels = row(need - 1)
        token = lambda i, p: jnp.concatenate(
            [row((i * n_core + p) * pieces + k) for k in range(pieces)], 1
        )
    else:
        labels = given[1][...].astype(F32)
        token = lambda i, p: given[0][i, p].astype(F32)
    label = lambda i: labels[:, i : i + 1].astype(I32)
    ids, times = label(0) * 64 + label(1), label(3)
    pick_time = (iota((n_all, buckets), 1) == times).astype(BF16)
    pick_row = (iota((n_all, conc_dev), 1) == ids - my_dp * conc_dev).astype(BF16)

    def owned_by(step):
        first = lax.rem(my_dp + n_dp - step, n_dp) * conc_dev
        return (ids >= first) & (ids < first + conc_dev)

    for p in range(n_core):
        shift, scale = dot(pick_time, mods[p][0]), 1.0 + dot(pick_time, mods[p][1])
        conc = scale * dot(pick_row, hats[p][...]) + shift
        first = jnp.where(
            owned_by(0), conc, jnp.where(owned_by(1), scale, jnp.where(owned_by(2), shift, 0.0))
        )
        lhs[p, 0:n_all] = first.astype(BF16)
        for i in range(per):
            rows_i = slice((1 + i) * n_all, (2 + i) * n_all)
            lhs[p, rows_i] = (scale * token(i, p) + shift).astype(BF16)
    slots = 1 + per
    kv_rows = kv_width // head_dim
    block = math.gcd(kv_width // chunks, 4 * head_dim)
    for at in range(0, kv_width, block):
        if at % (kv_width // chunks) == 0:
            for _, wait in weights:
                wait(at // (kv_width // chunks))
        cols = slice(at, at + block)
        terms = dot(lhs[0], weights[0][0][:, cols])
        for p in range(1, n_core):
            terms += dot(lhs[p], weights[p][0][:, cols])
        for s in range(slots):
            for r in range(block // head_dim):
                to = pl.ds(s * kv_rows + at // head_dim + r, n_all, stride=slots * kv_rows)
                flat[to, :] = terms[s * n_all : (s + 1) * n_all, r * head_dim : (r + 1) * head_dim]
    out[...] = flat[...].reshape(out.shape).astype(BF16)


def project(packets, mods, hats, weights, sizes, head_dim, tok_len):
    n_dp, n_chip, n_core = sizes
    width, kv_width = weights[0].shape
    per = tokens_per_dp(sizes, tok_len)
    need, rows = packet_rows(per, n_core, width)
    n_all = n_dp * n_chip
    slots, kv_rows = 1 + per, kv_width // head_dim
    chunks = 3
    given = [hold(packets)]
    if width % LANES:
        body = packets[:, : need - 1].reshape(n_all, -1)[:, : per * n_core * width]
        body = body.reshape(n_all, per, n_core, width).transpose(1, 2, 0, 3)
        given = [hold(body), hold(packets[:, need - 1])]
    (out,) = call(
        functools.partial(project_body, sizes, hats[0].shape[0], head_dim, per, chunks),
        [hold(x) for x in (*mods, *hats)] + [late(w, chunks) for w in weights] + given,
        [((n_all, slots * kv_rows, head_dim), BF16)],
        [
            pltpu.VMEM((n_core, slots * n_all, width), BF16),
            pltpu.VMEM((n_all * slots * kv_rows, head_dim), F32),
            pltpu.VMEM((n_all * rows, LANES), F32),
        ],
    )
    return out


def sample_body(sizes, tok_len, conc_dev, model_width, ins, outs, scratch):
    ids_ref, place_ref, time_ref, terms, bias, gain_ref, stat_ref = ins[:7]
    (q, q_wait), (g, g_wait) = ins[7:]
    (out,), (firsts, toks) = outs, scratch
    n_dp, n_chip, _ = sizes
    heads, _, img_len = stat_ref.shape
    kv_rows, head_dim = bias.shape
    per = tokens_per_dp(sizes, tok_len)
    scale = 1.0 / math.sqrt(head_dim)
    owner = jnp.int32(0)
    for d in range(1, n_dp):
        owner += (ids_ref[0] >= d * conc_dev).astype(I32)
    for d in range(n_dp):
        total = terms[d * n_chip].astype(F32)
        for s in range(1, n_chip):
            total += terms[d * n_chip + s].astype(F32)
        firsts[d * kv_rows : (d + 1) * kv_rows, :] = total[:kv_rows]
        for i in range(per):
            t = d * per + i
            if t < tok_len:
                toks[t * kv_rows : (t + 1) * kv_rows, :] = total[(1 + i) * kv_rows : (2 + i) * kv_rows]

    def gathered(step):
        at = lax.rem(owner + step, n_dp) * kv_rows
        return firsts[pl.ds(pl.multiple_of(at, 8), kv_rows), :]

    conc, scale_sum, shift_sum = gathered(0), gathered(1), gathered(2)
    full = conc + bias[...]
    raw_pos = full[:heads]
    inv_pos = lax.rsqrt(jnp.mean(raw_pos * raw_pos, -1, keepdims=True) + EPSILON)
    gain = gain_ref[...]
    at_pos = iota((tok_len, 1), 0) == place_ref[0]

    def text_rows(r):
        part = toks[pl.ds(r, tok_len, stride=kv_rows), :] + bias[r : r + 1, :]
        return jnp.where(at_pos, full[r : r + 1], part)

    keys, vals = [], []
    for h in range(heads):
        raw = text_rows(h)
        inv = lax.rsqrt(jnp.mean(raw * raw, -1, keepdims=True) + EPSILON)
        keys.append((raw * inv * gain).astype(BF16))
        vals.append(text_rows(heads + h).astype(BF16))
    q_wait(0)
    g_wait(0)
    cols = lambda h: slice(h * head_dim, (h + 1) * head_dim)
    shape = (heads, tok_len, img_len)
    s = jnp.concatenate([dot_nt(keys[h], q[:, cols(h)]) for h in range(heads)], 0)
    gv = jnp.concatenate([dot_nt(vals[h], g[:, cols(h)]) for h in range(heads)], 0)
    s, gv = s.reshape(shape) * scale, gv.reshape(shape)
    stats = stat_ref[...]
    top, total, weighted = stats[:, 0:1, :], stats[:, 1:2, :], stats[:, 2:3, :]
    new_top = jnp.maximum(top, jnp.max(s, 1, keepdims=True))
    e = jnp.exp(s - new_top)
    keep = jnp.exp(top - new_top)
    inv_total = 1.0 / (total * keep + jnp.sum(e, 1, keepdims=True))
    delta = (weighted * keep + jnp.sum(e * gv, 1, keepdims=True)) * inv_total
    here = iota((1, tok_len, 1), 1) == place_ref[0]
    p = jnp.sum(jnp.where(here, e, 0.0), 1, keepdims=True) * inv_total
    dscore = p * (jnp.sum(jnp.where(here, gv, 0.0), 1, keepdims=True) - delta)
    row = iota((1, 8, 1), 1)

    def two_rows(x):
        high = x.astype(BF16).astype(F32)
        return jnp.where(row == 0, high, jnp.where(row == 1, x - high, 0.0)).astype(BF16)

    p2, d2 = two_rows(p), two_rows(dscore)
    val_rows = [jnp.sum(dot(p2[h], g[:, cols(h)]), 0, keepdims=True) for h in range(heads)]
    key_rows = [jnp.sum(dot(d2[h], q[:, cols(h)]), 0, keepdims=True) for h in range(heads)]
    dn = jnp.concatenate(key_rows, 0) * scale * gain
    normed = raw_pos * inv_pos
    draw = inv_pos * (dn - normed * jnp.mean(dn * normed, -1, keepdims=True))
    dkv = jnp.concatenate([draw] + val_rows, 0)

    def total_of(x):
        return jnp.sum(jnp.sum(x, 0, keepdims=True), 1, keepdims=True) * (1.0 / model_width)

    means = split_bf16(total_of(dkv * scale_sum)) + split_bf16(total_of(dkv * (conc - shift_sum)))
    labels = (ids_ref[0] // 64, lax.rem(ids_ref[0], 64), time_ref[0])
    lane = iota((8, head_dim), 1)
    side = jnp.zeros((8, head_dim), F32)
    for i, x in enumerate(means + labels):
        side = jnp.where(lane == i, x.astype(F32), side)
    packet = jnp.concatenate([dkv, side], 0).astype(BF16)
    out[...] = jnp.broadcast_to(packet[None], out.shape)


def sample_part(ids, places, times, terms, bias, gain, stats, q, g, sizes, tok_len, conc_dev, model_width):
    kv_rows, head_dim = bias.shape
    per = tokens_per_dp(sizes, tok_len)
    (out,) = call(
        functools.partial(sample_body, sizes, tok_len, conc_dev, model_width),
        [scalar(ids), scalar(places), scalar(times), hold(terms), hold(bias), hold(gain), hold(stats)]
        + [late(q, 1), late(g, 1)],
        [((math.prod(sizes), kv_rows + 8, head_dim), BF16)],
        [
            pltpu.VMEM((sizes[0] * kv_rows, head_dim), F32),
            pltpu.VMEM((tok_len * kv_rows, head_dim), F32),
        ],
    )
    return out


def owner_body(chunks, ins, outs, scratch):
    packets, mod, hat, coef, (weight, wait) = ins
    (out,), (flat,) = outs, scratch
    n_dev, rows, head_dim = packets.shape
    conc_dev, buckets = hat.shape[0], mod.shape[1]
    parts = weight.shape[1] // head_dim
    first = lax.axis_index("dp") * conc_dev
    flat[...] = packets[...].reshape(n_dev * rows, head_dim).astype(F32)
    piece = lambda r: flat[pl.ds(r, n_dev, stride=rows), :]
    side = piece(parts)
    column = lambda i: side[:, i : i + 1]
    mean_1, mean_2 = column(0) + column(1), column(2) + column(3)
    mine = column(4).astype(I32) * 64 + column(5).astype(I32) - first
    times = column(6).astype(I32)
    scale = 1.0 + dot((iota((n_dev, buckets), 1) == times).astype(BF16), mod[1])
    one_hot = (iota((n_dev, conc_dev), 1) == mine).astype(BF16)
    conc = dot(one_hot, hat[...])
    size = parts // chunks
    grad = jnp.zeros(scale.shape, F32)
    for i in range(chunks):
        wait(i)
        dkv = jnp.concatenate([piece(r).astype(BF16) for r in range(i * size, (i + 1) * size)], 1)
        grad += dot_nt(dkv, weight[:, i * size * head_dim : (i + 1) * size * head_dim])
    grad = grad * scale - mean_1 - conc * mean_2
    high, low = split_bf16(grad)
    out[...] = (dot_tn(one_hot, high) + dot_tn(one_hot, low)) * coef[...]


def owner_part(packets, mod, hat, coef, weight):
    n_dev, rows, head_dim = packets.shape
    (out,) = call(
        functools.partial(owner_body, 3),
        [hold(x) for x in (packets, mod, hat, coef)] + [late(weight, 3)],
        [(hat.shape, F32)],
        [pltpu.VMEM((n_dev * rows, head_dim), F32)],
    )
    return out


def exchange(x, axes):
    return lax.all_to_all(x, axes, 0, 0, tiled=True)


def shards(
    txt_tokens,
    concept_table,
    concept_ids,
    positions,
    timesteps,
    counts,
    mod_table,
    kv_weight,
    kv_bias,
    key_gain,
    img_query,
    img_key,
    img_value,
    out_grad,
):
    sizes = tuple(lax.axis_size(a) for a in EVERYONE)
    n_dp, n_chip, n_core = sizes
    _, tok_len, model_width = txt_tokens.shape
    slice_width = kv_weight.shape[0]
    head_dim = key_gain.shape[0]
    conc_dev = concept_table.shape[0]

    def by_core(x):
        return [x] + [
            lax.ppermute(x, "core", [(i, i ^ s) for i in range(n_core)]) for s in range(1, n_core)
        ]

    packets = pack(concept_ids, positions, timesteps, txt_tokens[0], sizes, slice_width)
    packets = exchange(packets, CLASS)
    weights = by_core(kv_weight)
    hats, rstd, mods = table_part(concept_table, by_core(mod_table), slice_width, n_core)
    terms = project(packets, mods, hats, weights, sizes, head_dim, tok_len)
    terms = exchange(terms, CLASS)
    query, grad = img_query[0], out_grad[0]
    stats = image_part(query, img_key[0], img_value[0], grad, head_dim)
    packets = sample_part(
        concept_ids, positions, timesteps, terms, kv_bias.reshape(-1, head_dim), key_gain[None],
        stats, query, grad, sizes, tok_len, conc_dev, model_width,
    )
    packets = exchange(packets, EVERYONE)
    coef = rstd / counts.astype(F32)[:, None]
    return owner_part(packets, mods[0], hats[0], coef, kv_weight)


def solution(mesh):
    n_dp, n_fsdp = mesh.shape["dp"], mesh.shape["fsdp"]
    n_core = 2 if n_fsdp % 2 == 0 else 1
    fine = Mesh(mesh.devices.reshape(n_dp, n_fsdp // n_core, n_core), ("dp", "chip", "core"))
    fsdp = ("chip", "core")
    every = ("dp",) + fsdp
    placed = (
        P(every, None, None),
        P("dp", None),
        P(every),
        P(every),
        P(every),
        P("dp"),
        P(None, None, fsdp),
        P(fsdp, None),
        P(),
        P(),
        P(every, None, None),
        P(every, None, None),
        P(every, None, None),
        P(every, None, None),
    )
    return jax.shard_map(
        shards, mesh=fine, in_specs=placed, out_specs=P("dp", fsdp), check_vma=False
    )
```

```python
import functools
import math

import jax
import jax.numpy as jnp
from jax import lax
from jax.experimental import pallas as pl
from jax.experimental.pallas import tpu as pltpu
from jax.sharding import Mesh, PartitionSpec as P

EPSILON = 1e-06
BF16 = jnp.bfloat16
F32 = jnp.float32
I32 = jnp.int32
LANES = 128
MIB = 1024 * 1024
SPARE_ROWS = 128
ROOM_FOR_ONE = 53.25
NT = (((1,), (1,)), ((), ()))
TN = (((0,), (0,)), ((), ()))
EVERYONE = ("dp", "chip", "core")
CLASS = ("dp", "chip")


def dot(a, b):
    return jnp.dot(a, b, preferred_element_type=F32)


def dot_nt(a, b):
    return lax.dot_general(a, b, NT, preferred_element_type=F32)


def dot_tn(a, b):
    return lax.dot_general(a, b, TN, preferred_element_type=F32)


def split_bf16(x):
    high = x.astype(BF16)
    return high, (x - high.astype(F32)).astype(BF16)


def iota(shape, axis):
    return lax.broadcasted_iota(I32, shape, axis)


def hold(x):
    return ("hold", x)


def part(x, *cut):
    return ("part", x, cut)


def cut_shape(shape, cut):
    return tuple(c[1] for c in cut) + tuple(shape[len(cut) :])


def cut_index(cut):
    return tuple(pl.ds(*c) for c in cut)


def late(x, chunks, axis=1):
    return ("late", x, chunks, axis)


def scalar(x):
    return ("scalar", x)


def call(body, operands, results, scratch=(), vmem=63, flops=2_000_000_000):
    arrays = [o[1] for o in operands]
    shapes = [jax.ShapeDtypeStruct(*r[:2]) for r in results]
    cuts = [r[2] if len(r) > 2 else () for r in results]
    n_in, n_out = len(arrays), len(shapes)
    counts = [o[2] if o[0] == "late" else 1 for o in operands]
    offsets = [sum(counts[:i]) for i in range(n_in)]
    n_sems = sum(counts) + n_out

    def kernel(*refs):
        ins, outs = refs[:n_in], refs[n_in : n_in + n_out]
        held, made = refs[n_in + n_out : 2 * n_in + n_out], refs[2 * n_in + n_out : 2 * n_in + 2 * n_out]
        sems, extra = refs[2 * (n_in + n_out)], refs[2 * (n_in + n_out) + 1 :]

        def copies_of(i):
            o = operands[i]
            if o[0] == "part":
                return [pltpu.make_async_copy(ins[i].at[cut_index(o[2])], held[i], sems.at[offsets[i]])]
            if o[0] != "late" or o[2] == 1:
                return [pltpu.make_async_copy(ins[i], held[i], sems.at[offsets[i]])]
            size = o[1].shape[o[3]] // o[2]
            cut = lambda k: tuple([slice(None)] * o[3] + [pl.ds(k * size, size)])
            return [
                pltpu.make_async_copy(ins[i].at[cut(k)], held[i].at[cut(k)], sems.at[offsets[i] + k])
                for k in range(o[2])
            ]

        copies = [copies_of(i) for i in range(n_in)]
        first = [c for i in range(n_in) if operands[i][0] != "late" for c in copies[i]]
        then = [i for i in range(n_in) if operands[i][0] == "late"]
        for c in first:
            c.start()
        for k in range(max([counts[i] for i in then], default=0)):
            for i in then:
                if k < counts[i]:
                    copies[i][k].start()
        for c in first:
            c.wait()
        given = [
            (held[i], lambda k, i=i: copies[i][k].wait()) if operands[i][0] == "late" else held[i]
            for i in range(n_in)
        ]
        body(given, made, extra)
        final = [
            pltpu.make_async_copy(m, out.at[cut_index(c)] if c else out, sems.at[sum(counts) + k])
            for k, (m, out, c) in enumerate(zip(made, outs, cuts))
        ]
        for c in final:
            c.start()
        for c in final:
            c.wait()

    def place(o):
        shape = cut_shape(o[1].shape, o[2]) if o[0] == "part" else o[1].shape
        return (pltpu.SMEM if o[0] == "scalar" else pltpu.VMEM)(shape, o[1].dtype)

    return pl.pallas_call(
        kernel,
        in_specs=[pl.BlockSpec(memory_space=pltpu.HBM)] * n_in,
        out_specs=[pl.BlockSpec(memory_space=pltpu.HBM)] * n_out,
        out_shape=shapes,
        scratch_shapes=[place(o) for o in operands]
        + [pltpu.VMEM(cut_shape(s.shape, c), s.dtype) for s, c in zip(shapes, cuts)]
        + [pltpu.SemaphoreType.DMA((n_sems,))]
        + list(scratch),
        compiler_params=pltpu.CompilerParams(vmem_limit_bytes=int(vmem * MIB)),
        cost_estimate=pl.CostEstimate(flops=flops, bytes_accessed=1024, transcendentals=0),
    )(*arrays)


def normalise(x):
    d = x - jnp.mean(x, -1, keepdims=True)
    rstd = lax.rsqrt(jnp.mean(d * d, -1, keepdims=True) + EPSILON)
    return d * rstd, rstd


def tokens_per_dp(sizes, tok_len):
    return -(-tok_len // sizes[0])


def packet_rows(per, n_core, width):
    need = -(-per * n_core * width // LANES) + 1
    return need, -(-need // 16) * 16


def pack_body(sizes, width, per, ins, outs, scratch):
    n_dp, n_chip, n_core = sizes
    ids, times, tokens = ins
    (out,), (held, flat) = outs, scratch
    tok_len = tokens.shape[0]
    need, rows = packet_rows(per, n_core, width)
    pieces = width // LANES
    held[...] = normalise(tokens[...].astype(F32))[0]
    flat[...] = jnp.zeros(flat.shape, F32)
    lane = iota((1, LANES), 1)
    values = (ids[0] // 64, lax.rem(ids[0], 64), times[0])
    label = jnp.zeros((1, LANES), F32)
    for i, x in enumerate(values):
        label = jnp.where(lane == i, x.astype(F32), label)
    core = lax.axis_index("core")
    for d in range(n_dp):
        for chip in range(n_chip):
            base = (d * n_chip + chip) * rows
            flat[base + need - 1 : base + need, :] = label
            for i in range(per):
                t = d * per + i
                for p in range(n_core if t < tok_len else 0):
                    at = (chip * n_core + (core ^ p)) * width
                    for k in range(pieces):
                        r = base + (i * n_core + p) * pieces + k
                        lanes = pl.ds(pl.multiple_of(at + k * LANES, LANES), LANES)
                        flat[r : r + 1, :] = held[t : t + 1, lanes]
    out[...] = flat[...].reshape(out.shape).astype(BF16)


def hat_body(ins, outs, scratch):
    outs[0][...] = normalise(ins[0][...].astype(F32))[0].astype(BF16)


def pack(ids, times, tokens, sizes, width):
    n_dp, n_chip, n_core = sizes
    n_all = n_dp * n_chip
    tok_len, model_width = tokens.shape
    per = tokens_per_dp(sizes, tok_len)
    need, rows = packet_rows(per, n_core, width)
    if width % LANES == 0:
        (out,) = call(
            functools.partial(pack_body, sizes, width, per),
            [scalar(ids), scalar(times), hold(tokens)],
            [((n_all, rows, LANES), BF16)],
            [pltpu.VMEM(tokens.shape, F32), pltpu.VMEM((n_all * rows, LANES), F32)],
        )
        return out
    (hat,) = call(hat_body, [hold(tokens)], [(tokens.shape, BF16)])
    hat = jnp.pad(hat, ((0, n_dp * per - tok_len), (0, 0)))
    hat = hat.reshape(n_dp, per, n_chip, n_core, width)
    core = lax.axis_index("core")
    own = [lax.dynamic_index_in_dim(hat, core ^ p, 3, keepdims=False) for p in range(n_core)]
    body = jnp.stack(own, 3).transpose(0, 2, 1, 3, 4).reshape(n_all, -1)
    body = jnp.pad(body, ((0, 0), (0, (need - 1) * LANES - body.shape[1])))
    label = jnp.stack([ids[0] // 64, ids[0] % 64, times[0]]).astype(BF16)
    label = jnp.broadcast_to(jnp.pad(label, (0, LANES - 3))[None], (n_all, LANES))
    out = jnp.concatenate([body, label], 1).reshape(n_all, need, LANES)
    return jnp.pad(out, ((0, 0), (0, rows - need), (0, 0)))


def bank_rows(conc_dev, buckets):
    return conc_dev + 2 * buckets


def table_body(width, n_core, ins, outs, scratch):
    (table, wait), mods, parts = ins[0], ins[1 : 1 + n_core], ins[1 + n_core :]
    bank, rstd_out = outs
    chip, core = lax.axis_index("chip"), lax.axis_index("core")
    rows, buckets = table.shape[0], mods[0].shape[0]
    each = bank_rows(rows, buckets)
    for p, mod in enumerate(mods):
        x = mod[...].astype(F32)
        for i in range(2):
            at = p * each + rows + i * buckets
            bank[at : at + buckets, :] = x[:, i, :].astype(BF16)
    block = rows // 4
    for i in range(4):
        wait(i)
        here = slice(i * block, (i + 1) * block)
        x = table[here, :].astype(F32)
        mean = jnp.mean(x, -1, keepdims=True)
        d = x - mean
        rstd = lax.rsqrt(jnp.mean(d * d, -1, keepdims=True) + EPSILON)
        rstd_out[here, :] = rstd
        for p in range(n_core):
            if parts:
                piece = parts[p][here, :]
            else:
                at = pl.multiple_of((chip * n_core + (core ^ p)) * width, LANES)
                piece = table[here, pl.ds(at, width)]
            to = slice(p * each + i * block, p * each + (i + 1) * block)
            bank[to, :] = ((piece.astype(F32) - mean) * rstd).astype(BF16)


def table_part(table, mods, width, n_core):
    rows = table.shape[0]
    buckets = mods[0].shape[0]
    parts = []
    if width % LANES:
        chip, core = lax.axis_index("chip"), lax.axis_index("core")
        cut = lambda p: lax.dynamic_slice_in_dim(table, (chip * n_core + (core ^ p)) * width, width, 1)
        parts = [hold(cut(p)) for p in range(n_core)]
    used = n_core * bank_rows(rows, buckets)
    return call(
        functools.partial(table_body, width, n_core),
        [late(table, 4, 0)] + [hold(m) for m in mods] + parts,
        [((used + SPARE_ROWS, width), BF16, ((0, used),)), ((rows, 1), F32)],
    )


def image_body(head_dim, chunks, ins, outs, scratch):
    (q, _), (k, _), (v, _), (g, _) = ins
    (out,) = outs
    scale = 1.0 / math.sqrt(head_dim)
    heads = out.shape[0]
    for h in range(heads):
        if h % (heads // chunks) == 0:
            for _, wait in ins:
                wait(h // (heads // chunks))
        cols = slice(h * head_dim, (h + 1) * head_dim)
        s = dot_nt(k[:, cols], q[:, cols]) * scale
        gv = dot_nt(v[:, cols], g[:, cols])
        top = jnp.max(s, 0, keepdims=True)
        e = jnp.exp(s - top)
        out[h, 0:1, :] = top
        out[h, 1:2, :] = jnp.sum(e, 0, keepdims=True)
        out[h, 2:3, :] = jnp.sum(e * gv, 0, keepdims=True)


def image_part(q, k, v, g, head_dim):
    rows, width = q.shape
    heads = width // head_dim
    chunks = math.gcd(heads, 4)
    (out,) = call(
        functools.partial(image_body, head_dim, chunks),
        [late(x, chunks) for x in (q, k, v, g)],
        [((heads, 8 + SPARE_ROWS // 2, rows), F32, ((0, heads), (0, 8)))],
    )
    return out


def project_body(sizes, conc_dev, head_dim, per, chunks, ins, outs, scratch):
    n_dp, n_chip, n_core = sizes
    n_all = n_dp * n_chip
    bank, weights, given = ins[0], ins[1 : 1 + n_core], ins[1 + n_core :]
    (out,), (lhs, flat, flat_in) = outs, scratch
    width, kv_width = weights[0][0].shape
    each = bank.shape[0] // n_core
    buckets = (each - conc_dev) // 2
    my_dp = lax.axis_index("dp")
    if len(given) == 1:
        need, rows = packet_rows(per, n_core, width)
        pieces = width // LANES
        flat_in[...] = given[0][...].reshape(n_all * rows, LANES).astype(F32)
        row = lambda r: flat_in[pl.ds(r, n_all, stride=rows), :]
        labels = row(need - 1)
        token = lambda i, p: jnp.concatenate(
            [row((i * n_core + p) * pieces + k) for k in range(pieces)], 1
        )
    else:
        labels = given[1][...].astype(F32)
        token = lambda i, p: given[0][i, p].astype(F32)
    label = lambda i: labels[:, i : i + 1].astype(I32)
    ids, times = label(0) * 64 + label(1), label(2)
    pick_time = (iota((n_all, buckets), 1) == times).astype(BF16)
    pick_row = (iota((n_all, conc_dev), 1) == ids - my_dp * conc_dev).astype(BF16)

    def owned_by(step):
        first = lax.rem(my_dp + n_dp - step, n_dp) * conc_dev
        return (ids >= first) & (ids < first + conc_dev)

    for p in range(n_core):
        at = p * each + conc_dev
        shift = dot(pick_time, bank[at : at + buckets, :])
        scale = 1.0 + dot(pick_time, bank[at + buckets : at + 2 * buckets, :])
        conc = scale * dot(pick_row, bank[p * each : p * each + conc_dev, :]) + shift
        first = jnp.where(
            owned_by(0), conc, jnp.where(owned_by(1), scale, jnp.where(owned_by(2), shift, 0.0))
        )
        lhs[p, 0:n_all] = first.astype(BF16)
        for i in range(per):
            rows_i = slice((1 + i) * n_all, (2 + i) * n_all)
            lhs[p, rows_i] = (scale * token(i, p) + shift).astype(BF16)
    slots = 1 + per
    kv_rows = kv_width // head_dim
    block = math.gcd(kv_width // chunks, 4 * head_dim)
    for at in range(0, kv_width, block):
        if at % (kv_width // chunks) == 0:
            for _, wait in weights:
                wait(at // (kv_width // chunks))
        cols = slice(at, at + block)
        terms = dot(lhs[0], weights[0][0][:, cols])
        for p in range(1, n_core):
            terms += dot(lhs[p], weights[p][0][:, cols])
        for s in range(slots):
            for r in range(block // head_dim):
                to = pl.ds(s * kv_rows + at // head_dim + r, n_all, stride=slots * kv_rows)
                flat[to, :] = terms[s * n_all : (s + 1) * n_all, r * head_dim : (r + 1) * head_dim]
    out[...] = flat[...].reshape(out.shape).astype(BF16)


def project(packets, bank, conc_dev, weights, sizes, head_dim, tok_len):
    n_dp, n_chip, n_core = sizes
    width, kv_width = weights[0].shape
    per = tokens_per_dp(sizes, tok_len)
    need, rows = packet_rows(per, n_core, width)
    n_all = n_dp * n_chip
    slots, kv_rows = 1 + per, kv_width // head_dim
    chunks = 3
    given = [hold(packets)]
    if width % LANES:
        body = packets[:, : need - 1].reshape(n_all, -1)[:, : per * n_core * width]
        body = body.reshape(n_all, per, n_core, width).transpose(1, 2, 0, 3)
        given = [hold(body), hold(packets[:, need - 1])]
    (out,) = call(
        functools.partial(project_body, sizes, conc_dev, head_dim, per, chunks),
        [part(bank, (0, bank.shape[0] - SPARE_ROWS))] + [late(w, chunks) for w in weights] + given,
        [((n_all, slots * kv_rows, head_dim), BF16)],
        [
            pltpu.VMEM((n_core, slots * n_all, width), BF16),
            pltpu.VMEM((n_all * slots * kv_rows, head_dim), F32),
            pltpu.VMEM((n_all * rows, LANES), F32),
        ],
        vmem=ROOM_FOR_ONE,
    )
    return out


def sample_body(sizes, tok_len, conc_dev, model_width, ins, outs, scratch):
    ids_ref, place_ref, time_ref, terms, bias, gain_ref, stat_ref = ins[:7]
    (q, q_wait), (g, g_wait) = ins[7:]
    (out,), (firsts, toks) = outs, scratch
    n_dp, n_chip, _ = sizes
    heads, _, img_len = stat_ref.shape
    kv_rows, head_dim = bias.shape
    per = tokens_per_dp(sizes, tok_len)
    scale = 1.0 / math.sqrt(head_dim)
    owner = jnp.int32(0)
    for d in range(1, n_dp):
        owner += (ids_ref[0] >= d * conc_dev).astype(I32)
    for d in range(n_dp):
        total = terms[d * n_chip].astype(F32)
        for s in range(1, n_chip):
            total += terms[d * n_chip + s].astype(F32)
        firsts[d * kv_rows : (d + 1) * kv_rows, :] = total[:kv_rows]
        for i in range(per):
            t = d * per + i
            if t < tok_len:
                toks[t * kv_rows : (t + 1) * kv_rows, :] = total[(1 + i) * kv_rows : (2 + i) * kv_rows]

    def gathered(step):
        at = lax.rem(owner + step, n_dp) * kv_rows
        return firsts[pl.ds(pl.multiple_of(at, 8), kv_rows), :]

    conc, scale_sum, shift_sum = gathered(0), gathered(1), gathered(2)
    full = conc + bias[...]
    raw_pos = full[:heads]
    inv_pos = lax.rsqrt(jnp.mean(raw_pos * raw_pos, -1, keepdims=True) + EPSILON)
    gain = gain_ref[...]
    at_pos = iota((tok_len, 1), 0) == place_ref[0]

    def text_rows(r):
        part = toks[pl.ds(r, tok_len, stride=kv_rows), :] + bias[r : r + 1, :]
        return jnp.where(at_pos, full[r : r + 1], part)

    keys, vals = [], []
    for h in range(heads):
        raw = text_rows(h)
        inv = lax.rsqrt(jnp.mean(raw * raw, -1, keepdims=True) + EPSILON)
        keys.append((raw * inv * gain).astype(BF16))
        vals.append(text_rows(heads + h).astype(BF16))
    q_wait(0)
    g_wait(0)
    cols = lambda h: slice(h * head_dim, (h + 1) * head_dim)
    shape = (heads, tok_len, img_len)
    s = jnp.concatenate([dot_nt(keys[h], q[:, cols(h)]) for h in range(heads)], 0)
    gv = jnp.concatenate([dot_nt(vals[h], g[:, cols(h)]) for h in range(heads)], 0)
    s, gv = s.reshape(shape) * scale, gv.reshape(shape)
    stats = stat_ref[...]
    top, total, weighted = stats[:, 0:1, :], stats[:, 1:2, :], stats[:, 2:3, :]
    new_top = jnp.maximum(top, jnp.max(s, 1, keepdims=True))
    e = jnp.exp(s - new_top)
    keep = jnp.exp(top - new_top)
    inv_total = 1.0 / (total * keep + jnp.sum(e, 1, keepdims=True))
    delta = (weighted * keep + jnp.sum(e * gv, 1, keepdims=True)) * inv_total
    here = iota((1, tok_len, 1), 1) == place_ref[0]
    p = jnp.sum(jnp.where(here, e, 0.0), 1, keepdims=True) * inv_total
    dscore = p * (jnp.sum(jnp.where(here, gv, 0.0), 1, keepdims=True) - delta)
    row = iota((1, 8, 1), 1)

    def two_rows(x):
        high = x.astype(BF16).astype(F32)
        return jnp.where(row == 0, high, jnp.where(row == 1, x - high, 0.0)).astype(BF16)

    p2, d2 = two_rows(p), two_rows(dscore)
    val_rows = [jnp.sum(dot(p2[h], g[:, cols(h)]), 0, keepdims=True) for h in range(heads)]
    key_rows = [jnp.sum(dot(d2[h], q[:, cols(h)]), 0, keepdims=True) for h in range(heads)]
    dn = jnp.concatenate(key_rows, 0) * scale * gain
    normed = raw_pos * inv_pos
    draw = inv_pos * (dn - normed * jnp.mean(dn * normed, -1, keepdims=True))
    dkv = jnp.concatenate([draw] + val_rows, 0)

    def total_of(x):
        return jnp.sum(jnp.sum(x, 0, keepdims=True), 1, keepdims=True) * (1.0 / model_width)

    means = split_bf16(total_of(dkv * scale_sum)) + split_bf16(total_of(dkv * (conc - shift_sum)))
    labels = (ids_ref[0] // 64, lax.rem(ids_ref[0], 64), time_ref[0])
    lane = iota((8, head_dim), 1)
    side = jnp.zeros((8, head_dim), F32)
    for i, x in enumerate(means + labels):
        side = jnp.where(lane == i, x.astype(F32), side)
    packet = jnp.concatenate([dkv, side], 0).astype(BF16)
    out[...] = jnp.broadcast_to(packet[None], out.shape)


def sample_part(ids, places, times, terms, bias, gain, stats, q, g, sizes, tok_len, conc_dev, model_width):
    kv_rows, head_dim = bias.shape
    per = tokens_per_dp(sizes, tok_len)
    (out,) = call(
        functools.partial(sample_body, sizes, tok_len, conc_dev, model_width),
        [scalar(ids), scalar(places), scalar(times), hold(terms), hold(bias), hold(gain)]
        + [part(stats, (0, stats.shape[0]), (0, 8))]
        + [late(q, 1), late(g, 1)],
        [((sizes[0] * sizes[1], kv_rows + 8, head_dim), BF16)],
        [
            pltpu.VMEM((sizes[0] * kv_rows, head_dim), F32),
            pltpu.VMEM((tok_len * kv_rows, head_dim), F32),
        ],
        vmem=ROOM_FOR_ONE,
    )
    return out


def owner_body(chunks, ins, outs, scratch):
    bank, coef, (weight, wait), packets = *ins[:3], ins[3:]
    (out,), (flat,) = outs, scratch
    n_each, rows, head_dim = packets[0].shape
    n_dev = n_each * len(packets)
    conc_dev = coef.shape[0]
    buckets = (bank.shape[0] - conc_dev) // 2
    parts = weight.shape[1] // head_dim
    first = lax.axis_index("dp") * conc_dev
    for i, x in enumerate(packets):
        flat[i * n_each * rows : (i + 1) * n_each * rows, :] = (
            x[...].reshape(n_each * rows, head_dim).astype(F32)
        )
    piece = lambda r: flat[pl.ds(r, n_dev, stride=rows), :]
    side = piece(parts)
    column = lambda i: side[:, i : i + 1]
    mean_1, mean_2 = column(0) + column(1), column(2) + column(3)
    mine = column(4).astype(I32) * 64 + column(5).astype(I32) - first
    times = column(6).astype(I32)
    scale = 1.0 + dot((iota((n_dev, buckets), 1) == times).astype(BF16), bank[conc_dev + buckets :, :])
    one_hot = (iota((n_dev, conc_dev), 1) == mine).astype(BF16)
    conc = dot(one_hot, bank[0:conc_dev, :])
    size = parts // chunks
    grad = jnp.zeros(scale.shape, F32)
    for i in range(chunks):
        wait(i)
        dkv = jnp.concatenate([piece(r).astype(BF16) for r in range(i * size, (i + 1) * size)], 1)
        grad += dot_nt(dkv, weight[:, i * size * head_dim : (i + 1) * size * head_dim])
    grad = grad * scale - mean_1 - conc * mean_2
    high, low = split_bf16(grad)
    out[...] = (dot_tn(one_hot, high) + dot_tn(one_hot, low)) * coef[...]


def owner_part(packets, bank, n_core, coef, weight):
    each = (bank.shape[0] - SPARE_ROWS) // n_core
    n_each, rows, head_dim = packets[0].shape
    n_dev = n_each * len(packets)
    (out,) = call(
        functools.partial(owner_body, 3),
        [part(bank, (0, each)), hold(coef), late(weight, 3)] + [hold(x) for x in packets],
        [((coef.shape[0], weight.shape[0]), F32)],
        [pltpu.VMEM((n_dev * rows, head_dim), F32)],
        vmem=ROOM_FOR_ONE,
    )
    return out


def exchange(x, axes):
    return lax.all_to_all(x, axes, 0, 0, tiled=True)


def shards(
    txt_tokens,
    concept_table,
    concept_ids,
    positions,
    timesteps,
    counts,
    mod_table,
    kv_weight,
    kv_bias,
    key_gain,
    img_query,
    img_key,
    img_value,
    out_grad,
):
    sizes = tuple(lax.axis_size(a) for a in EVERYONE)
    n_dp, n_chip, n_core = sizes
    _, tok_len, model_width = txt_tokens.shape
    slice_width = kv_weight.shape[0]
    head_dim = key_gain.shape[0]
    conc_dev = concept_table.shape[0]

    def by_core(x):
        return [x] + [
            lax.ppermute(x, "core", [(i, i ^ s) for i in range(n_core)]) for s in range(1, n_core)
        ]

    packets = pack(concept_ids, timesteps, txt_tokens[0], sizes, slice_width)
    packets = exchange(packets, CLASS)
    weights = by_core(kv_weight)
    bank, rstd = table_part(concept_table, by_core(mod_table), slice_width, n_core)
    terms = project(packets, bank, conc_dev, weights, sizes, head_dim, tok_len)
    terms = exchange(terms, CLASS)
    query, grad = img_query[0], out_grad[0]
    stats = image_part(query, img_key[0], img_value[0], grad, head_dim)
    packets = sample_part(
        concept_ids, positions, timesteps, terms, kv_bias.reshape(-1, head_dim), key_gain[None],
        stats, query, grad, sizes, tok_len, conc_dev, model_width,
    )
    packets = by_core(exchange(packets, CLASS))
    coef = rstd / counts.astype(F32)[:, None]
    return owner_part(packets, bank, n_core, coef, kv_weight)


def solution(mesh):
    n_dp, n_fsdp = mesh.shape["dp"], mesh.shape["fsdp"]
    n_core = 2 if n_fsdp % 2 == 0 else 1
    fine = Mesh(mesh.devices.reshape(n_dp, n_fsdp // n_core, n_core), ("dp", "chip", "core"))
    fsdp = ("chip", "core")
    every = ("dp",) + fsdp
    placed = (
        P(every, None, None),
        P("dp", None),
        P(every),
        P(every),
        P(every),
        P("dp"),
        P(None, None, fsdp),
        P(fsdp, None),
        P(),
        P(),
        P(every, None, None),
        P(every, None, None),
        P(every, None, None),
        P(every, None, None),
    )
    return jax.shard_map(
        shards, mesh=fine, in_specs=placed, out_specs=P("dp", fsdp), check_vma=False
    )
```

```python
import functools
import math

import jax
import jax.numpy as jnp
from jax import lax
from jax.experimental import pallas as pl
from jax.experimental.pallas import tpu as pltpu
from jax.sharding import Mesh, PartitionSpec as P

EPSILON = 1e-06
BF16 = jnp.bfloat16
F32 = jnp.float32
I32 = jnp.int32
LANES = 128
MIB = 1024 * 1024
SPARE_ROWS = 128
GRANT = dict(table=51.6, image=51.8, project=52.7, sample=51.8, owner=53.25)
NT = (((1,), (1,)), ((), ()))
TN = (((0,), (0,)), ((), ()))
EVERYONE = ("dp", "chip", "core")
CLASS = ("dp", "chip")


def dot(a, b):
    return jnp.dot(a, b, preferred_element_type=F32)


def dot_nt(a, b):
    return lax.dot_general(a, b, NT, preferred_element_type=F32)


def dot_tn(a, b):
    return lax.dot_general(a, b, TN, preferred_element_type=F32)


def split_bf16(x):
    high = x.astype(BF16)
    return high, (x - high.astype(F32)).astype(BF16)


def iota(shape, axis):
    return lax.broadcasted_iota(I32, shape, axis)


def hold(x):
    return ("hold", x)


def part(x, *cut):
    return ("part", x, cut)


def cut_shape(shape, cut):
    return tuple(c[1] for c in cut) + tuple(shape[len(cut) :])


def cut_index(cut):
    return tuple(pl.ds(*c) for c in cut)


def late(x, chunks, axis=1):
    return ("late", x, chunks, axis)


def scalar(x):
    return ("scalar", x)


def direct(x):
    return ("direct", x)


def call(body, operands, results, scratch=(), vmem=63, flops=2_000_000_000):
    arrays = [o[1] for o in operands]
    shapes = [jax.ShapeDtypeStruct(*r[:2]) for r in results]
    cuts = [r[2] if len(r) > 2 else () for r in results]
    n_in, n_out = len(arrays), len(shapes)
    counts = [o[2] if o[0] == "late" else 1 for o in operands]
    offsets = [sum(counts[:i]) for i in range(n_in)]
    n_sems = sum(counts) + n_out

    def kernel(*refs):
        ins, outs = refs[:n_in], refs[n_in : n_in + n_out]
        spare, made = refs[n_in + n_out : 2 * n_in + n_out], refs[2 * n_in + n_out : 2 * n_in + 2 * n_out]
        held = [r if o[0] == "direct" else h for o, r, h in zip(operands, ins, spare)]
        sems, extra = refs[2 * (n_in + n_out)], refs[2 * (n_in + n_out) + 1 :]

        def copies_of(i):
            o = operands[i]
            if o[0] == "direct":
                return []
            if o[0] == "part":
                return [pltpu.make_async_copy(ins[i].at[cut_index(o[2])], held[i], sems.at[offsets[i]])]
            if o[0] != "late" or o[2] == 1:
                return [pltpu.make_async_copy(ins[i], held[i], sems.at[offsets[i]])]
            size = o[1].shape[o[3]] // o[2]
            cut = lambda k: tuple([slice(None)] * o[3] + [pl.ds(k * size, size)])
            return [
                pltpu.make_async_copy(ins[i].at[cut(k)], held[i].at[cut(k)], sems.at[offsets[i] + k])
                for k in range(o[2])
            ]

        copies = [copies_of(i) for i in range(n_in)]
        first = [c for i in range(n_in) if operands[i][0] != "late" for c in copies[i]]
        then = [i for i in range(n_in) if operands[i][0] == "late"]
        for c in first:
            c.start()
        for k in range(max([counts[i] for i in then], default=0)):
            for i in then:
                if k < counts[i]:
                    copies[i][k].start()
        for c in first:
            c.wait()
        given = [
            (held[i], lambda k, i=i: copies[i][k].wait()) if operands[i][0] == "late" else held[i]
            for i in range(n_in)
        ]
        body(given, made, extra)
        final = [
            pltpu.make_async_copy(m, out.at[cut_index(c)] if c else out, sems.at[sum(counts) + k])
            for k, (m, out, c) in enumerate(zip(made, outs, cuts))
        ]
        for c in final:
            c.start()
        for c in final:
            c.wait()

    def place(o):
        shape = cut_shape(o[1].shape, o[2]) if o[0] == "part" else o[1].shape
        shape = (8, LANES) if o[0] == "direct" else shape
        return (pltpu.SMEM if o[0] == "scalar" else pltpu.VMEM)(shape, o[1].dtype)

    return pl.pallas_call(
        kernel,
        in_specs=[
            pl.BlockSpec(memory_space=pltpu.VMEM if o[0] == "direct" else pltpu.HBM) for o in operands
        ],
        out_specs=[pl.BlockSpec(memory_space=pltpu.HBM)] * n_out,
        out_shape=shapes,
        scratch_shapes=[place(o) for o in operands]
        + [pltpu.VMEM(cut_shape(s.shape, c), s.dtype) for s, c in zip(shapes, cuts)]
        + [pltpu.SemaphoreType.DMA((n_sems,))]
        + list(scratch),
        compiler_params=pltpu.CompilerParams(vmem_limit_bytes=int(vmem * MIB)),
        cost_estimate=pl.CostEstimate(flops=flops, bytes_accessed=1024, transcendentals=0),
    )(*arrays)


def normalise(x):
    d = x - jnp.mean(x, -1, keepdims=True)
    rstd = lax.rsqrt(jnp.mean(d * d, -1, keepdims=True) + EPSILON)
    return d * rstd, rstd


def tokens_per_dp(sizes, tok_len):
    return -(-tok_len // sizes[0])


def packet_rows(per, n_core, width):
    need = -(-per * n_core * width // LANES) + 1
    return need, -(-need // 16) * 16


def pack_body(sizes, width, per, ins, outs, scratch):
    n_dp, n_chip, n_core = sizes
    ids, times, tokens = ins
    (out,), (held, flat) = outs, scratch
    tok_len = tokens.shape[0]
    need, rows = packet_rows(per, n_core, width)
    pieces = width // LANES
    held[...] = normalise(tokens[...].astype(F32))[0]
    flat[...] = jnp.zeros(flat.shape, F32)
    lane = iota((1, LANES), 1)
    values = (ids[0] // 64, lax.rem(ids[0], 64), times[0])
    label = jnp.zeros((1, LANES), F32)
    for i, x in enumerate(values):
        label = jnp.where(lane == i, x.astype(F32), label)
    core = lax.axis_index("core")
    for d in range(n_dp):
        for chip in range(n_chip):
            base = (d * n_chip + chip) * rows
            flat[base + need - 1 : base + need, :] = label
            for i in range(per):
                t = d * per + i
                for p in range(n_core if t < tok_len else 0):
                    at = (chip * n_core + (core ^ p)) * width
                    for k in range(pieces):
                        r = base + (i * n_core + p) * pieces + k
                        lanes = pl.ds(pl.multiple_of(at + k * LANES, LANES), LANES)
                        flat[r : r + 1, :] = held[t : t + 1, lanes]
    out[...] = flat[...].reshape(out.shape).astype(BF16)


def hat_body(ins, outs, scratch):
    outs[0][...] = normalise(ins[0][...].astype(F32))[0].astype(BF16)


def pack(ids, times, tokens, sizes, width):
    n_dp, n_chip, n_core = sizes
    n_all = n_dp * n_chip
    tok_len, model_width = tokens.shape
    per = tokens_per_dp(sizes, tok_len)
    need, rows = packet_rows(per, n_core, width)
    if width % LANES == 0:
        (out,) = call(
            functools.partial(pack_body, sizes, width, per),
            [scalar(ids), scalar(times), hold(tokens)],
            [((n_all, rows, LANES), BF16)],
            [pltpu.VMEM(tokens.shape, F32), pltpu.VMEM((n_all * rows, LANES), F32)],
        )
        return out
    (hat,) = call(hat_body, [hold(tokens)], [(tokens.shape, BF16)])
    hat = jnp.pad(hat, ((0, n_dp * per - tok_len), (0, 0)))
    hat = hat.reshape(n_dp, per, n_chip, n_core, width)
    core = lax.axis_index("core")
    own = [lax.dynamic_index_in_dim(hat, core ^ p, 3, keepdims=False) for p in range(n_core)]
    body = jnp.stack(own, 3).transpose(0, 2, 1, 3, 4).reshape(n_all, -1)
    body = jnp.pad(body, ((0, 0), (0, (need - 1) * LANES - body.shape[1])))
    label = jnp.stack([ids[0] // 64, ids[0] % 64, times[0]]).astype(BF16)
    label = jnp.broadcast_to(jnp.pad(label, (0, LANES - 3))[None], (n_all, LANES))
    out = jnp.concatenate([body, label], 1).reshape(n_all, need, LANES)
    return jnp.pad(out, ((0, 0), (0, rows - need), (0, 0)))


def bank_rows(conc_dev, buckets):
    return conc_dev + 2 * buckets


def table_body(width, n_core, ins, outs, scratch):
    (table, wait), mods, parts = ins[0], ins[1 : 1 + n_core], ins[1 + n_core :]
    bank, rstd_out = outs
    chip, core = lax.axis_index("chip"), lax.axis_index("core")
    rows, buckets = table.shape[0], mods[0].shape[0]
    each = bank_rows(rows, buckets)
    for p, mod in enumerate(mods):
        x = mod[...].astype(F32)
        for i in range(2):
            at = p * each + rows + i * buckets
            bank[at : at + buckets, :] = x[:, i, :].astype(BF16)
    block = rows // 2
    for i in range(2):
        wait(i)
        here = slice(i * block, (i + 1) * block)
        x = table[here, :].astype(F32)
        mean = jnp.mean(x, -1, keepdims=True)
        d = x - mean
        rstd = lax.rsqrt(jnp.mean(d * d, -1, keepdims=True) + EPSILON)
        rstd_out[here, :] = rstd
        for p in range(n_core):
            if parts:
                piece = parts[p][here, :]
            else:
                at = pl.multiple_of((chip * n_core + (core ^ p)) * width, LANES)
                piece = table[here, pl.ds(at, width)]
            to = slice(p * each + i * block, p * each + (i + 1) * block)
            bank[to, :] = ((piece.astype(F32) - mean) * rstd).astype(BF16)


def table_part(table, mods, width, n_core):
    rows = table.shape[0]
    buckets = mods[0].shape[0]
    parts = []
    if width % LANES:
        chip, core = lax.axis_index("chip"), lax.axis_index("core")
        cut = lambda p: lax.dynamic_slice_in_dim(table, (chip * n_core + (core ^ p)) * width, width, 1)
        parts = [hold(cut(p)) for p in range(n_core)]
    used = n_core * bank_rows(rows, buckets)
    return call(
        functools.partial(table_body, width, n_core),
        [late(table, 2, 0)] + [hold(m) for m in mods] + parts,
        [((used + SPARE_ROWS, width), BF16, ((0, used),)), ((rows, 1), F32)],
        vmem=GRANT["table"],
    )


def image_body(head_dim, chunks, ins, outs, scratch):
    (q, _), (k, _), (v, _), (g, _) = ins
    (out,) = outs
    scale = 1.0 / math.sqrt(head_dim)
    heads = out.shape[0]
    for h in range(heads):
        if h % (heads // chunks) == 0:
            for _, wait in ins:
                wait(h // (heads // chunks))
        cols = slice(h * head_dim, (h + 1) * head_dim)
        s = dot_nt(k[:, cols], q[:, cols]) * scale
        gv = dot_nt(v[:, cols], g[:, cols])
        top = jnp.max(s, 0, keepdims=True)
        e = jnp.exp(s - top)
        out[h, 0:1, :] = top
        out[h, 1:2, :] = jnp.sum(e, 0, keepdims=True)
        out[h, 2:3, :] = jnp.sum(e * gv, 0, keepdims=True)


def image_part(q, k, v, g, head_dim):
    rows, width = q.shape
    heads = width // head_dim
    chunks = math.gcd(heads, 2)
    (out,) = call(
        functools.partial(image_body, head_dim, chunks),
        [late(x, chunks) for x in (q, k, v, g)],
        [((heads, 8 + SPARE_ROWS, rows), F32, ((0, heads), (0, 8)))],
        vmem=GRANT["image"],
    )
    return out


def project_body(sizes, conc_dev, head_dim, per, chunks, ins, outs, scratch):
    n_dp, n_chip, n_core = sizes
    n_all = n_dp * n_chip
    bank, weights, given = ins[0], ins[1 : 1 + n_core], ins[1 + n_core :]
    (out,), (lhs, flat, flat_in) = outs, scratch
    width, kv_width = weights[0][0].shape
    each = bank.shape[0] // n_core
    buckets = (each - conc_dev) // 2
    my_dp = lax.axis_index("dp")
    if len(given) == 1:
        need, rows = packet_rows(per, n_core, width)
        pieces = width // LANES
        flat_in[...] = given[0][...].reshape(n_all * rows, LANES).astype(F32)
        row = lambda r: flat_in[pl.ds(r, n_all, stride=rows), :]
        labels = row(need - 1)
        token = lambda i, p: jnp.concatenate(
            [row((i * n_core + p) * pieces + k) for k in range(pieces)], 1
        )
    else:
        labels = given[1][...].astype(F32)
        token = lambda i, p: given[0][i, p].astype(F32)
    label = lambda i: labels[:, i : i + 1].astype(I32)
    ids, times = label(0) * 64 + label(1), label(2)
    pick_time = (iota((n_all, buckets), 1) == times).astype(BF16)
    pick_row = (iota((n_all, conc_dev), 1) == ids - my_dp * conc_dev).astype(BF16)

    def owned_by(step):
        first = lax.rem(my_dp + n_dp - step, n_dp) * conc_dev
        return (ids >= first) & (ids < first + conc_dev)

    for p in range(n_core):
        at = p * each + conc_dev
        shift = dot(pick_time, bank[at : at + buckets, :])
        scale = 1.0 + dot(pick_time, bank[at + buckets : at + 2 * buckets, :])
        conc = scale * dot(pick_row, bank[p * each : p * each + conc_dev, :]) + shift
        first = jnp.where(
            owned_by(0), conc, jnp.where(owned_by(1), scale, jnp.where(owned_by(2), shift, 0.0))
        )
        lhs[p, 0:n_all] = first.astype(BF16)
        for i in range(per):
            rows_i = slice((1 + i) * n_all, (2 + i) * n_all)
            lhs[p, rows_i] = (scale * token(i, p) + shift).astype(BF16)
    slots = 1 + per
    kv_rows = kv_width // head_dim
    block = math.gcd(kv_width // chunks, 4 * head_dim)
    for at in range(0, kv_width, block):
        if at % (kv_width // chunks) == 0:
            for _, wait in weights:
                wait(at // (kv_width // chunks))
        cols = slice(at, at + block)
        terms = dot(lhs[0], weights[0][0][:, cols])
        for p in range(1, n_core):
            terms += dot(lhs[p], weights[p][0][:, cols])
        for s in range(slots):
            for r in range(block // head_dim):
                to = pl.ds(s * kv_rows + at // head_dim + r, n_all, stride=slots * kv_rows)
                flat[to, :] = terms[s * n_all : (s + 1) * n_all, r * head_dim : (r + 1) * head_dim]
    out[...] = flat[...].reshape(out.shape).astype(BF16)


def project(packets, bank, conc_dev, weights, sizes, head_dim, tok_len):
    n_dp, n_chip, n_core = sizes
    width, kv_width = weights[0].shape
    per = tokens_per_dp(sizes, tok_len)
    need, rows = packet_rows(per, n_core, width)
    n_all = n_dp * n_chip
    slots, kv_rows = 1 + per, kv_width // head_dim
    chunks = 3
    given = [hold(packets)]
    if width % LANES:
        body = packets[:, : need - 1].reshape(n_all, -1)[:, : per * n_core * width]
        body = body.reshape(n_all, per, n_core, width).transpose(1, 2, 0, 3)
        given = [hold(body), hold(packets[:, need - 1])]
    (out,) = call(
        functools.partial(project_body, sizes, conc_dev, head_dim, per, chunks),
        [part(bank, (0, bank.shape[0] - SPARE_ROWS))] + [late(w, chunks) for w in weights] + given,
        [((n_all, slots * kv_rows, head_dim), BF16)],
        [
            pltpu.VMEM((n_core, slots * n_all, width), BF16),
            pltpu.VMEM((n_all * slots * kv_rows, head_dim), F32),
            pltpu.VMEM((n_all * rows, LANES), F32),
        ],
        vmem=GRANT["project"],
    )
    return out


def sample_body(sizes, tok_len, conc_dev, model_width, ins, outs, scratch):
    ids_ref, place_ref, time_ref, terms, bias, gain_ref, stat_ref = ins[:7]
    q, g = ins[7:]
    (out,), (firsts, toks) = outs, scratch
    n_dp, n_chip, _ = sizes
    heads, _, img_len = stat_ref.shape
    kv_rows, head_dim = bias.shape
    per = tokens_per_dp(sizes, tok_len)
    scale = 1.0 / math.sqrt(head_dim)
    owner = jnp.int32(0)
    for d in range(1, n_dp):
        owner += (ids_ref[0] >= d * conc_dev).astype(I32)
    for d in range(n_dp):
        total = terms[d * n_chip].astype(F32)
        for s in range(1, n_chip):
            total += terms[d * n_chip + s].astype(F32)
        firsts[d * kv_rows : (d + 1) * kv_rows, :] = total[:kv_rows]
        for i in range(per):
            t = d * per + i
            if t < tok_len:
                toks[t * kv_rows : (t + 1) * kv_rows, :] = total[(1 + i) * kv_rows : (2 + i) * kv_rows]

    def gathered(step):
        at = lax.rem(owner + step, n_dp) * kv_rows
        return firsts[pl.ds(pl.multiple_of(at, 8), kv_rows), :]

    conc, scale_sum, shift_sum = gathered(0), gathered(1), gathered(2)
    full = conc + bias[...]
    raw_pos = full[:heads]
    inv_pos = lax.rsqrt(jnp.mean(raw_pos * raw_pos, -1, keepdims=True) + EPSILON)
    gain = gain_ref[...]
    at_pos = iota((tok_len, 1), 0) == place_ref[0]

    def text_rows(r):
        part = toks[pl.ds(r, tok_len, stride=kv_rows), :] + bias[r : r + 1, :]
        return jnp.where(at_pos, full[r : r + 1], part)

    keys, vals = [], []
    for h in range(heads):
        raw = text_rows(h)
        inv = lax.rsqrt(jnp.mean(raw * raw, -1, keepdims=True) + EPSILON)
        keys.append((raw * inv * gain).astype(BF16))
        vals.append(text_rows(heads + h).astype(BF16))
    cols = lambda h: slice(h * head_dim, (h + 1) * head_dim)
    shape = (heads, tok_len, img_len)
    s = jnp.concatenate([dot_nt(keys[h], q[:, cols(h)]) for h in range(heads)], 0)
    gv = jnp.concatenate([dot_nt(vals[h], g[:, cols(h)]) for h in range(heads)], 0)
    s, gv = s.reshape(shape) * scale, gv.reshape(shape)
    stats = stat_ref[...]
    top, total, weighted = stats[:, 0:1, :], stats[:, 1:2, :], stats[:, 2:3, :]
    new_top = jnp.maximum(top, jnp.max(s, 1, keepdims=True))
    e = jnp.exp(s - new_top)
    keep = jnp.exp(top - new_top)
    inv_total = 1.0 / (total * keep + jnp.sum(e, 1, keepdims=True))
    delta = (weighted * keep + jnp.sum(e * gv, 1, keepdims=True)) * inv_total
    here = iota((1, tok_len, 1), 1) == place_ref[0]
    p = jnp.sum(jnp.where(here, e, 0.0), 1, keepdims=True) * inv_total
    dscore = p * (jnp.sum(jnp.where(here, gv, 0.0), 1, keepdims=True) - delta)
    row = iota((1, 8, 1), 1)

    def two_rows(x):
        high = x.astype(BF16).astype(F32)
        return jnp.where(row == 0, high, jnp.where(row == 1, x - high, 0.0)).astype(BF16)

    p2, d2 = two_rows(p), two_rows(dscore)
    val_rows = [jnp.sum(dot(p2[h], g[:, cols(h)]), 0, keepdims=True) for h in range(heads)]
    key_rows = [jnp.sum(dot(d2[h], q[:, cols(h)]), 0, keepdims=True) for h in range(heads)]
    dn = jnp.concatenate(key_rows, 0) * scale * gain
    normed = raw_pos * inv_pos
    draw = inv_pos * (dn - normed * jnp.mean(dn * normed, -1, keepdims=True))
    dkv = jnp.concatenate([draw] + val_rows, 0)

    def total_of(x):
        return jnp.sum(jnp.sum(x, 0, keepdims=True), 1, keepdims=True) * (1.0 / model_width)

    means = split_bf16(total_of(dkv * scale_sum)) + split_bf16(total_of(dkv * (conc - shift_sum)))
    labels = (ids_ref[0] // 64, lax.rem(ids_ref[0], 64), time_ref[0])
    lane = iota((8, head_dim), 1)
    side = jnp.zeros((8, head_dim), F32)
    for i, x in enumerate(means + labels):
        side = jnp.where(lane == i, x.astype(F32), side)
    packet = jnp.concatenate([dkv, side], 0).astype(BF16)
    out[...] = jnp.broadcast_to(packet[None], out.shape)


def sample_part(ids, places, times, terms, bias, gain, stats, q, g, sizes, tok_len, conc_dev, model_width):
    kv_rows, head_dim = bias.shape
    per = tokens_per_dp(sizes, tok_len)
    (out,) = call(
        functools.partial(sample_body, sizes, tok_len, conc_dev, model_width),
        [scalar(ids), scalar(places), scalar(times), hold(terms), hold(bias), hold(gain)]
        + [part(stats, (0, stats.shape[0]), (0, 8))]
        + [direct(q), direct(g)],
        [((sizes[0] * sizes[1], kv_rows + 8, head_dim), BF16)],
        [
            pltpu.VMEM((sizes[0] * kv_rows, head_dim), F32),
            pltpu.VMEM((tok_len * kv_rows, head_dim), F32),
        ],
        vmem=GRANT["sample"],
    )
    return out


def owner_body(chunks, ins, outs, scratch):
    bank, coef, (weight, wait), packets = *ins[:3], ins[3:]
    (out,), (flat,) = outs, scratch
    n_each, rows, head_dim = packets[0].shape
    n_dev = n_each * len(packets)
    conc_dev = coef.shape[0]
    buckets = (bank.shape[0] - conc_dev) // 2
    parts = weight.shape[1] // head_dim
    first = lax.axis_index("dp") * conc_dev
    for i, x in enumerate(packets):
        flat[i * n_each * rows : (i + 1) * n_each * rows, :] = (
            x[...].reshape(n_each * rows, head_dim).astype(F32)
        )
    piece = lambda r: flat[pl.ds(r, n_dev, stride=rows), :]
    side = piece(parts)
    column = lambda i: side[:, i : i + 1]
    mean_1, mean_2 = column(0) + column(1), column(2) + column(3)
    mine = column(4).astype(I32) * 64 + column(5).astype(I32) - first
    times = column(6).astype(I32)
    scale = 1.0 + dot((iota((n_dev, buckets), 1) == times).astype(BF16), bank[conc_dev + buckets :, :])
    one_hot = (iota((n_dev, conc_dev), 1) == mine).astype(BF16)
    conc = dot(one_hot, bank[0:conc_dev, :])
    size = parts // chunks
    grad = jnp.zeros(scale.shape, F32)
    for i in range(chunks):
        wait(i)
        dkv = jnp.concatenate([piece(r).astype(BF16) for r in range(i * size, (i + 1) * size)], 1)
        grad += dot_nt(dkv, weight[:, i * size * head_dim : (i + 1) * size * head_dim])
    grad = grad * scale - mean_1 - conc * mean_2
    high, low = split_bf16(grad)
    out[...] = (dot_tn(one_hot, high) + dot_tn(one_hot, low)) * coef[...]


def owner_part(packets, bank, n_core, coef, weight):
    each = (bank.shape[0] - SPARE_ROWS) // n_core
    n_each, rows, head_dim = packets[0].shape
    n_dev = n_each * len(packets)
    (out,) = call(
        functools.partial(owner_body, 3),
        [part(bank, (0, each)), hold(coef), late(weight, 3)] + [hold(x) for x in packets],
        [((coef.shape[0], weight.shape[0]), F32)],
        [pltpu.VMEM((n_dev * rows, head_dim), F32)],
        vmem=GRANT["owner"],
    )
    return out


def exchange(x, axes):
    return lax.all_to_all(x, axes, 0, 0, tiled=True)


def shards(
    txt_tokens,
    concept_table,
    concept_ids,
    positions,
    timesteps,
    counts,
    mod_table,
    kv_weight,
    kv_bias,
    key_gain,
    img_query,
    img_key,
    img_value,
    out_grad,
):
    sizes = tuple(lax.axis_size(a) for a in EVERYONE)
    n_dp, n_chip, n_core = sizes
    _, tok_len, model_width = txt_tokens.shape
    slice_width = kv_weight.shape[0]
    head_dim = key_gain.shape[0]
    conc_dev = concept_table.shape[0]

    def by_core(x):
        return [x] + [
            lax.ppermute(x, "core", [(i, i ^ s) for i in range(n_core)]) for s in range(1, n_core)
        ]

    packets = pack(concept_ids, timesteps, txt_tokens[0], sizes, slice_width)
    packets = exchange(packets, CLASS)
    weights = by_core(kv_weight)
    bank, rstd = table_part(concept_table, by_core(mod_table), slice_width, n_core)
    terms = project(packets, bank, conc_dev, weights, sizes, head_dim, tok_len)
    terms = exchange(terms, CLASS)
    query, grad = img_query[0], out_grad[0]
    stats = image_part(query, img_key[0], img_value[0], grad, head_dim)
    packets = sample_part(
        concept_ids, positions, timesteps, terms, kv_bias.reshape(-1, head_dim), key_gain[None],
        stats, query, grad, sizes, tok_len, conc_dev, model_width,
    )
    packets = by_core(exchange(packets, CLASS))
    coef = rstd / counts.astype(F32)[:, None]
    return owner_part(packets, bank, n_core, coef, kv_weight)


def solution(mesh):
    n_dp, n_fsdp = mesh.shape["dp"], mesh.shape["fsdp"]
    n_core = 2 if n_fsdp % 2 == 0 else 1
    fine = Mesh(mesh.devices.reshape(n_dp, n_fsdp // n_core, n_core), ("dp", "chip", "core"))
    fsdp = ("chip", "core")
    every = ("dp",) + fsdp
    placed = (
        P(every, None, None),
        P("dp", None),
        P(every),
        P(every),
        P(every),
        P("dp"),
        P(None, None, fsdp),
        P(fsdp, None),
        P(),
        P(),
        P(every, None, None),
        P(every, None, None),
        P(every, None, None),
        P(every, None, None),
    )
    return jax.shard_map(
        shards, mesh=fine, in_specs=placed, out_specs=P("dp", fsdp), check_vma=False
    )
```

```python
import functools
import math

import jax
import jax.numpy as jnp
from jax import lax
from jax.experimental import pallas as pl
from jax.experimental.pallas import tpu as pltpu
from jax.sharding import Mesh, PartitionSpec as P

EPSILON = 1e-06
BF16 = jnp.bfloat16
F32 = jnp.float32
I32 = jnp.int32
LANES = 128
MIB = 1024 * 1024
SPARE_ROWS = 128
GRANT = dict(table=51.6, image=51.8, project=52.7, sample=51.8, owner=53.25)
NT = (((1,), (1,)), ((), ()))
TN = (((0,), (0,)), ((), ()))
EVERYONE = ("dp", "chip", "core")
CLASS = ("dp", "chip")


def dot(a, b):
    return jnp.dot(a, b, preferred_element_type=F32)


def dot_nt(a, b):
    return lax.dot_general(a, b, NT, preferred_element_type=F32)


def dot_tn(a, b):
    return lax.dot_general(a, b, TN, preferred_element_type=F32)


def split_bf16(x):
    high = x.astype(BF16)
    return high, (x - high.astype(F32)).astype(BF16)


def iota(shape, axis):
    return lax.broadcasted_iota(I32, shape, axis)


def hold(x):
    return ("hold", x)


def part(x, *cut):
    return ("part", x, cut)


def late_part(x, *cut):
    return ("late_part", x, cut)


def cut_shape(shape, cut):
    return tuple(c[1] for c in cut) + tuple(shape[len(cut) :])


def cut_index(cut):
    return tuple(pl.ds(*c) for c in cut)


def late(x, chunks, axis=1):
    return ("late", x, chunks, axis)


def scalar(x):
    return ("scalar", x)


def direct(x):
    return ("direct", x)


def call(body, operands, results, scratch=(), vmem=63, flops=2_000_000_000):
    arrays = [o[1] for o in operands]
    shapes = [jax.ShapeDtypeStruct(*r[:2]) for r in results]
    cuts = [r[2] if len(r) > 2 else () for r in results]
    n_in, n_out = len(arrays), len(shapes)
    counts = [o[2] if o[0] == "late" else 1 for o in operands]
    offsets = [sum(counts[:i]) for i in range(n_in)]
    n_sems = sum(counts) + n_out

    def kernel(*refs):
        ins, outs = refs[:n_in], refs[n_in : n_in + n_out]
        spare, made = refs[n_in + n_out : 2 * n_in + n_out], refs[2 * n_in + n_out : 2 * n_in + 2 * n_out]
        held = [r if o[0] in ("direct", "scalar") else h for o, r, h in zip(operands, ins, spare)]
        sems, extra = refs[2 * (n_in + n_out)], refs[2 * (n_in + n_out) + 1 :]

        def copies_of(i):
            o = operands[i]
            if o[0] in ("direct", "scalar"):
                return []
            if o[0] in ("part", "late_part"):
                return [pltpu.make_async_copy(ins[i].at[cut_index(o[2])], held[i], sems.at[offsets[i]])]
            if o[0] != "late" or o[2] == 1:
                return [pltpu.make_async_copy(ins[i], held[i], sems.at[offsets[i]])]
            size = o[1].shape[o[3]] // o[2]
            cut = lambda k: tuple([slice(None)] * o[3] + [pl.ds(k * size, size)])
            return [
                pltpu.make_async_copy(ins[i].at[cut(k)], held[i].at[cut(k)], sems.at[offsets[i] + k])
                for k in range(o[2])
            ]

        copies = [copies_of(i) for i in range(n_in)]
        is_late = [o[0] in ("late", "late_part") for o in operands]
        first = [c for i in range(n_in) if not is_late[i] for c in copies[i]]
        then = [i for i in range(n_in) if is_late[i]]
        for c in first:
            c.start()
        for k in range(max([counts[i] for i in then], default=0)):
            for i in then:
                if k < counts[i]:
                    copies[i][k].start()
        for c in first:
            c.wait()
        given = [
            (held[i], lambda k, i=i: copies[i][k].wait()) if is_late[i] else held[i]
            for i in range(n_in)
        ]
        body(given, made, extra)
        final = [
            pltpu.make_async_copy(m, out.at[cut_index(c)] if c else out, sems.at[sum(counts) + k])
            for k, (m, out, c) in enumerate(zip(made, outs, cuts))
        ]
        for c in final:
            c.start()
        for c in final:
            c.wait()

    def spare_of(o):
        shape = cut_shape(o[1].shape, o[2]) if o[0] in ("part", "late_part") else o[1].shape
        return pltpu.VMEM((8, LANES) if o[0] in ("direct", "scalar") else shape, o[1].dtype)

    spaces = {"direct": pltpu.VMEM, "scalar": pltpu.SMEM}
    return pl.pallas_call(
        kernel,
        in_specs=[
            pl.BlockSpec(memory_space=spaces.get(o[0], pltpu.HBM)) for o in operands
        ],
        out_specs=[pl.BlockSpec(memory_space=pltpu.HBM)] * n_out,
        out_shape=shapes,
        scratch_shapes=[spare_of(o) for o in operands]
        + [pltpu.VMEM(cut_shape(s.shape, c), s.dtype) for s, c in zip(shapes, cuts)]
        + [pltpu.SemaphoreType.DMA((n_sems,))]
        + list(scratch),
        compiler_params=pltpu.CompilerParams(vmem_limit_bytes=int(vmem * MIB)),
        cost_estimate=pl.CostEstimate(flops=flops, bytes_accessed=1024, transcendentals=0),
    )(*arrays)


def normalise(x):
    d = x - jnp.mean(x, -1, keepdims=True)
    rstd = lax.rsqrt(jnp.mean(d * d, -1, keepdims=True) + EPSILON)
    return d * rstd, rstd


def tokens_per_dp(sizes, tok_len):
    return -(-tok_len // sizes[0])


def packet_rows(per, n_core, width):
    need = -(-per * n_core * width // LANES) + 1
    return need, -(-need // 16) * 16


def pack_body(sizes, width, per, ins, outs, scratch):
    n_dp, n_chip, n_core = sizes
    ids, times, tokens = ins
    (out,), (held, flat) = outs, scratch
    tok_len = tokens.shape[0]
    need, rows = packet_rows(per, n_core, width)
    pieces = width // LANES
    held[...] = normalise(tokens[...].astype(F32))[0]
    flat[...] = jnp.zeros(flat.shape, F32)
    lane = iota((1, LANES), 1)
    values = (ids[0] // 64, lax.rem(ids[0], 64), times[0])
    label = jnp.zeros((1, LANES), F32)
    for i, x in enumerate(values):
        label = jnp.where(lane == i, x.astype(F32), label)
    core = lax.axis_index("core")
    for d in range(n_dp):
        for chip in range(n_chip):
            base = (d * n_chip + chip) * rows
            flat[base + need - 1 : base + need, :] = label
            for i in range(per):
                t = d * per + i
                for p in range(n_core if t < tok_len else 0):
                    at = (chip * n_core + (core ^ p)) * width
                    for k in range(pieces):
                        r = base + (i * n_core + p) * pieces + k
                        lanes = pl.ds(pl.multiple_of(at + k * LANES, LANES), LANES)
                        flat[r : r + 1, :] = held[t : t + 1, lanes]
    out[...] = flat[...].reshape(out.shape).astype(BF16)


def hat_body(ins, outs, scratch):
    outs[0][...] = normalise(ins[0][...].astype(F32))[0].astype(BF16)


def pack(ids, times, tokens, sizes, width):
    n_dp, n_chip, n_core = sizes
    n_all = n_dp * n_chip
    tok_len, model_width = tokens.shape
    per = tokens_per_dp(sizes, tok_len)
    need, rows = packet_rows(per, n_core, width)
    if width % LANES == 0:
        (out,) = call(
            functools.partial(pack_body, sizes, width, per),
            [scalar(ids), scalar(times), hold(tokens)],
            [((n_all, rows, LANES), BF16)],
            [pltpu.VMEM(tokens.shape, F32), pltpu.VMEM((n_all * rows, LANES), F32)],
        )
        return out
    (hat,) = call(hat_body, [hold(tokens)], [(tokens.shape, BF16)])
    hat = jnp.pad(hat, ((0, n_dp * per - tok_len), (0, 0)))
    hat = hat.reshape(n_dp, per, n_chip, n_core, width)
    core = lax.axis_index("core")
    own = [lax.dynamic_index_in_dim(hat, core ^ p, 3, keepdims=False) for p in range(n_core)]
    body = jnp.stack(own, 3).transpose(0, 2, 1, 3, 4).reshape(n_all, -1)
    body = jnp.pad(body, ((0, 0), (0, (need - 1) * LANES - body.shape[1])))
    label = jnp.stack([ids[0] // 64, ids[0] % 64, times[0]]).astype(BF16)
    label = jnp.broadcast_to(jnp.pad(label, (0, LANES - 3))[None], (n_all, LANES))
    out = jnp.concatenate([body, label], 1).reshape(n_all, need, LANES)
    return jnp.pad(out, ((0, 0), (0, rows - need), (0, 0)))


def bank_rows(conc_dev, buckets):
    return conc_dev + 2 * buckets


def table_body(width, n_core, ins, outs, scratch):
    (table, wait), mods, parts = ins[0], ins[1 : 1 + n_core], ins[1 + n_core :]
    bank, rstd_out = outs
    chip, core = lax.axis_index("chip"), lax.axis_index("core")
    rows, buckets = table.shape[0], mods[0].shape[0]
    each = bank_rows(rows, buckets)
    for p, mod in enumerate(mods):
        x = mod[...].astype(F32)
        for i in range(2):
            at = p * each + rows + i * buckets
            bank[at : at + buckets, :] = x[:, i, :].astype(BF16)
    block = rows // 2
    for i in range(2):
        wait(i)
        here = slice(i * block, (i + 1) * block)
        x = table[here, :].astype(F32)
        mean = jnp.mean(x, -1, keepdims=True)
        d = x - mean
        rstd = lax.rsqrt(jnp.mean(d * d, -1, keepdims=True) + EPSILON)
        rstd_out[here, :] = rstd
        for p in range(n_core):
            if parts:
                piece = parts[p][here, :]
            else:
                at = pl.multiple_of((chip * n_core + (core ^ p)) * width, LANES)
                piece = table[here, pl.ds(at, width)]
            to = slice(p * each + i * block, p * each + (i + 1) * block)
            bank[to, :] = ((piece.astype(F32) - mean) * rstd).astype(BF16)


def table_part(table, mods, width, n_core):
    rows = table.shape[0]
    buckets = mods[0].shape[0]
    parts = []
    if width % LANES:
        chip, core = lax.axis_index("chip"), lax.axis_index("core")
        cut = lambda p: lax.dynamic_slice_in_dim(table, (chip * n_core + (core ^ p)) * width, width, 1)
        parts = [hold(cut(p)) for p in range(n_core)]
    used = n_core * bank_rows(rows, buckets)
    return call(
        functools.partial(table_body, width, n_core),
        [late(table, 2, 0)] + [hold(m) for m in mods] + parts,
        [((used + SPARE_ROWS, width), BF16, ((0, used),)), ((rows, 1), F32)],
        vmem=GRANT["table"],
    )


def image_body(head_dim, chunks, ins, outs, scratch):
    (q, _), (k, _), (v, _), (g, _) = ins
    (out,) = outs
    scale = 1.0 / math.sqrt(head_dim)
    heads = out.shape[0]
    for h in range(heads):
        if h % (heads // chunks) == 0:
            for _, wait in ins:
                wait(h // (heads // chunks))
        cols = slice(h * head_dim, (h + 1) * head_dim)
        s = dot_nt(k[:, cols], q[:, cols]) * scale
        gv = dot_nt(v[:, cols], g[:, cols])
        top = jnp.max(s, 0, keepdims=True)
        e = jnp.exp(s - top)
        out[h, 0:1, :] = top
        out[h, 1:2, :] = jnp.sum(e, 0, keepdims=True)
        out[h, 2:3, :] = jnp.sum(e * gv, 0, keepdims=True)


def image_part(q, k, v, g, head_dim):
    rows, width = q.shape
    heads = width // head_dim
    chunks = math.gcd(heads, 2)
    (out,) = call(
        functools.partial(image_body, head_dim, chunks),
        [late(x, chunks) for x in (q, k, v, g)],
        [((heads, 8 + SPARE_ROWS, rows), F32, ((0, heads), (0, 8)))],
        vmem=GRANT["image"],
    )
    return out


def project_body(sizes, conc_dev, head_dim, per, chunks, ins, outs, scratch):
    n_dp, n_chip, n_core = sizes
    n_all = n_dp * n_chip
    bank, weights, given = ins[0], ins[1 : 1 + n_core], ins[1 + n_core :]
    (out,), (lhs, flat, flat_in) = outs, scratch
    width, kv_width = weights[0][0].shape
    each = (bank.shape[0] - SPARE_ROWS) // n_core
    buckets = (each - conc_dev) // 2
    my_dp = lax.axis_index("dp")
    if len(given) == 1:
        need, rows = packet_rows(per, n_core, width)
        pieces = width // LANES
        flat_in[...] = given[0][...].reshape(n_all * rows, LANES).astype(F32)
        row = lambda r: flat_in[pl.ds(r, n_all, stride=rows), :]
        labels = row(need - 1)
        token = lambda i, p: jnp.concatenate(
            [row((i * n_core + p) * pieces + k) for k in range(pieces)], 1
        )
    else:
        labels = given[1][...].astype(F32)
        token = lambda i, p: given[0][i, p].astype(F32)
    label = lambda i: labels[:, i : i + 1].astype(I32)
    ids, times = label(0) * 64 + label(1), label(2)
    pick_time = (iota((n_all, buckets), 1) == times).astype(BF16)
    pick_row = (iota((n_all, conc_dev), 1) == ids - my_dp * conc_dev).astype(BF16)

    def owned_by(step):
        first = lax.rem(my_dp + n_dp - step, n_dp) * conc_dev
        return (ids >= first) & (ids < first + conc_dev)

    for p in range(n_core):
        at = p * each + conc_dev
        shift = dot(pick_time, bank[at : at + buckets, :])
        scale = 1.0 + dot(pick_time, bank[at + buckets : at + 2 * buckets, :])
        conc = scale * dot(pick_row, bank[p * each : p * each + conc_dev, :]) + shift
        first = jnp.where(
            owned_by(0), conc, jnp.where(owned_by(1), scale, jnp.where(owned_by(2), shift, 0.0))
        )
        lhs[p, 0:n_all] = first.astype(BF16)
        for i in range(per):
            rows_i = slice((1 + i) * n_all, (2 + i) * n_all)
            lhs[p, rows_i] = (scale * token(i, p) + shift).astype(BF16)
    slots = 1 + per
    kv_rows = kv_width // head_dim
    block = math.gcd(kv_width // chunks, 4 * head_dim)
    for at in range(0, kv_width, block):
        if at % (kv_width // chunks) == 0:
            for _, wait in weights:
                wait(at // (kv_width // chunks))
        cols = slice(at, at + block)
        terms = dot(lhs[0], weights[0][0][:, cols])
        for p in range(1, n_core):
            terms += dot(lhs[p], weights[p][0][:, cols])
        for s in range(slots):
            for r in range(block // head_dim):
                to = pl.ds(s * kv_rows + at // head_dim + r, n_all, stride=slots * kv_rows)
                flat[to, :] = terms[s * n_all : (s + 1) * n_all, r * head_dim : (r + 1) * head_dim]
    out[...] = flat[...].reshape(out.shape).astype(BF16)


def project(packets, bank, conc_dev, weights, sizes, head_dim, tok_len):
    n_dp, n_chip, n_core = sizes
    width, kv_width = weights[0].shape
    per = tokens_per_dp(sizes, tok_len)
    need, rows = packet_rows(per, n_core, width)
    n_all = n_dp * n_chip
    slots, kv_rows = 1 + per, kv_width // head_dim
    chunks = 3
    given = [direct(packets)]
    if width % LANES:
        body = packets[:, : need - 1].reshape(n_all, -1)[:, : per * n_core * width]
        body = body.reshape(n_all, per, n_core, width).transpose(1, 2, 0, 3)
        given = [hold(body), hold(packets[:, need - 1])]
    (out,) = call(
        functools.partial(project_body, sizes, conc_dev, head_dim, per, chunks),
        [direct(bank)] + [late(w, chunks) for w in weights] + given,
        [((n_all, slots * kv_rows, head_dim), BF16)],
        [
            pltpu.VMEM((n_core, slots * n_all, width), BF16),
            pltpu.VMEM((n_all * slots * kv_rows, head_dim), F32),
            pltpu.VMEM((n_all * rows, LANES), F32),
        ],
        vmem=GRANT["project"],
    )
    return out


def sample_body(sizes, tok_len, conc_dev, model_width, ins, outs, scratch):
    ids_ref, place_ref, time_ref, terms, bias, gain_ref, (stat_ref, stat_wait) = ins[:7]
    q, g = ins[7:]
    (out,), (firsts, toks) = outs, scratch
    n_dp, n_chip, _ = sizes
    heads, _, img_len = stat_ref.shape
    kv_rows, head_dim = bias.shape
    per = tokens_per_dp(sizes, tok_len)
    scale = 1.0 / math.sqrt(head_dim)
    owner = jnp.int32(0)
    for d in range(1, n_dp):
        owner += (ids_ref[0] >= d * conc_dev).astype(I32)
    for d in range(n_dp):
        total = terms[d * n_chip].astype(F32)
        for s in range(1, n_chip):
            total += terms[d * n_chip + s].astype(F32)
        firsts[d * kv_rows : (d + 1) * kv_rows, :] = total[:kv_rows]
        for i in range(per):
            t = d * per + i
            if t < tok_len:
                toks[t * kv_rows : (t + 1) * kv_rows, :] = total[(1 + i) * kv_rows : (2 + i) * kv_rows]

    def gathered(step):
        at = lax.rem(owner + step, n_dp) * kv_rows
        return firsts[pl.ds(pl.multiple_of(at, 8), kv_rows), :]

    conc, scale_sum, shift_sum = gathered(0), gathered(1), gathered(2)
    full = conc + bias[...]
    raw_pos = full[:heads]
    inv_pos = lax.rsqrt(jnp.mean(raw_pos * raw_pos, -1, keepdims=True) + EPSILON)
    gain = gain_ref[...]
    at_pos = iota((tok_len, 1), 0) == place_ref[0]

    def text_rows(r):
        part = toks[pl.ds(r, tok_len, stride=kv_rows), :] + bias[r : r + 1, :]
        return jnp.where(at_pos, full[r : r + 1], part)

    keys, vals = [], []
    for h in range(heads):
        raw = text_rows(h)
        inv = lax.rsqrt(jnp.mean(raw * raw, -1, keepdims=True) + EPSILON)
        keys.append((raw * inv * gain).astype(BF16))
        vals.append(text_rows(heads + h).astype(BF16))
    cols = lambda h: slice(h * head_dim, (h + 1) * head_dim)
    shape = (heads, tok_len, img_len)
    s = jnp.concatenate([dot_nt(keys[h], q[:, cols(h)]) for h in range(heads)], 0)
    gv = jnp.concatenate([dot_nt(vals[h], g[:, cols(h)]) for h in range(heads)], 0)
    s, gv = s.reshape(shape) * scale, gv.reshape(shape)
    stat_wait(0)
    stats = stat_ref[...]
    top, total, weighted = stats[:, 0:1, :], stats[:, 1:2, :], stats[:, 2:3, :]
    new_top = jnp.maximum(top, jnp.max(s, 1, keepdims=True))
    e = jnp.exp(s - new_top)
    keep = jnp.exp(top - new_top)
    inv_total = 1.0 / (total * keep + jnp.sum(e, 1, keepdims=True))
    delta = (weighted * keep + jnp.sum(e * gv, 1, keepdims=True)) * inv_total
    here = iota((1, tok_len, 1), 1) == place_ref[0]
    p = jnp.sum(jnp.where(here, e, 0.0), 1, keepdims=True) * inv_total
    dscore = p * (jnp.sum(jnp.where(here, gv, 0.0), 1, keepdims=True) - delta)
    row = iota((1, 8, 1), 1)

    def two_rows(x):
        high = x.astype(BF16).astype(F32)
        return jnp.where(row == 0, high, jnp.where(row == 1, x - high, 0.0)).astype(BF16)

    p2, d2 = two_rows(p), two_rows(dscore)
    val_rows = [jnp.sum(dot(p2[h], g[:, cols(h)]), 0, keepdims=True) for h in range(heads)]
    key_rows = [jnp.sum(dot(d2[h], q[:, cols(h)]), 0, keepdims=True) for h in range(heads)]
    dn = jnp.concatenate(key_rows, 0) * scale * gain
    normed = raw_pos * inv_pos
    draw = inv_pos * (dn - normed * jnp.mean(dn * normed, -1, keepdims=True))
    dkv = jnp.concatenate([draw] + val_rows, 0)

    def total_of(x):
        return jnp.sum(jnp.sum(x, 0, keepdims=True), 1, keepdims=True) * (1.0 / model_width)

    means = split_bf16(total_of(dkv * scale_sum)) + split_bf16(total_of(dkv * (conc - shift_sum)))
    labels = (ids_ref[0] // 64, lax.rem(ids_ref[0], 64), time_ref[0])
    lane = iota((8, head_dim), 1)
    side = jnp.zeros((8, head_dim), F32)
    for i, x in enumerate(means + labels):
        side = jnp.where(lane == i, x.astype(F32), side)
    packet = jnp.concatenate([dkv, side], 0).astype(BF16)
    out[...] = jnp.broadcast_to(packet[None], out.shape)


def sample_part(ids, places, times, terms, bias, gain, stats, q, g, sizes, tok_len, conc_dev, model_width):
    kv_rows, head_dim = bias.shape
    per = tokens_per_dp(sizes, tok_len)
    (out,) = call(
        functools.partial(sample_body, sizes, tok_len, conc_dev, model_width),
        [scalar(ids), scalar(places), scalar(times), direct(terms), direct(bias), direct(gain)]
        + [late_part(stats, (0, stats.shape[0]), (0, 8))]
        + [direct(q), direct(g)],
        [((sizes[0] * sizes[1], kv_rows + 8, head_dim), BF16)],
        [
            pltpu.VMEM((sizes[0] * kv_rows, head_dim), F32),
            pltpu.VMEM((tok_len * kv_rows, head_dim), F32),
        ],
        vmem=GRANT["sample"],
    )
    return out


def owner_body(chunks, ins, outs, scratch):
    (bank, bank_wait), (coef, coef_wait), (weight, wait), packets = *ins[:3], ins[3:]
    (out,), (flat,) = outs, scratch
    n_each, rows, head_dim = packets[0].shape
    n_dev = n_each * len(packets)
    conc_dev = coef.shape[0]
    buckets = (bank.shape[0] - conc_dev) // 2
    parts = weight.shape[1] // head_dim
    first = lax.axis_index("dp") * conc_dev
    for i, x in enumerate(packets):
        flat[i * n_each * rows : (i + 1) * n_each * rows, :] = (
            x[...].reshape(n_each * rows, head_dim).astype(F32)
        )
    piece = lambda r: flat[pl.ds(r, n_dev, stride=rows), :]
    side = piece(parts)
    column = lambda i: side[:, i : i + 1]
    mean_1, mean_2 = column(0) + column(1), column(2) + column(3)
    side_rows = side.T
    row = lambda i: side_rows[i : i + 1, :].astype(I32)
    ids_row = row(4) * 64 + row(5) - first
    owned = (iota((conc_dev, n_dev), 0) == ids_row).astype(BF16)
    owned = jnp.concatenate([owned, owned], 1)
    mine = column(4).astype(I32) * 64 + column(5).astype(I32) - first
    times = column(6).astype(I32)
    bank_wait(0)
    scale = 1.0 + dot((iota((n_dev, buckets), 1) == times).astype(BF16), bank[conc_dev + buckets :, :])
    one_hot = (iota((n_dev, conc_dev), 1) == mine).astype(BF16)
    offset = mean_1 + dot(one_hot, bank[0:conc_dev, :]) * mean_2
    coef_wait(0)
    factor = jnp.broadcast_to(coef[...], out.shape)
    size = parts // chunks
    grad = jnp.zeros((n_dev, weight.shape[0]), F32)
    for i in range(chunks):
        dkv = jnp.concatenate([piece(r).astype(BF16) for r in range(i * size, (i + 1) * size)], 1)
        wait(i)
        grad += dot_nt(dkv, weight[:, i * size * head_dim : (i + 1) * size * head_dim])
    high, low = split_bf16(grad * scale - offset)
    out[...] = dot(owned, jnp.concatenate([high, low], 0)) * factor


def owner_part(packets, bank, n_core, coef, weight):
    each = (bank.shape[0] - SPARE_ROWS) // n_core
    n_each, rows, head_dim = packets[0].shape
    n_dev = n_each * len(packets)
    (out,) = call(
        functools.partial(owner_body, 3),
        [late_part(bank, (0, each)), late(coef, 1), late(weight, 3)] + [direct(x) for x in packets],
        [((coef.shape[0], weight.shape[0]), F32)],
        [pltpu.VMEM((n_dev * rows, head_dim), F32)],
        vmem=GRANT["owner"],
    )
    return out


def exchange(x, axes):
    return lax.all_to_all(x, axes, 0, 0, tiled=True)


def shards(
    txt_tokens,
    concept_table,
    concept_ids,
    positions,
    timesteps,
    counts,
    mod_table,
    kv_weight,
    kv_bias,
    key_gain,
    img_query,
    img_key,
    img_value,
    out_grad,
):
    sizes = tuple(lax.axis_size(a) for a in EVERYONE)
    n_dp, n_chip, n_core = sizes
    _, tok_len, model_width = txt_tokens.shape
    slice_width = kv_weight.shape[0]
    head_dim = key_gain.shape[0]
    conc_dev = concept_table.shape[0]

    def by_core(x):
        return [x] + [
            lax.ppermute(x, "core", [(i, i ^ s) for i in range(n_core)]) for s in range(1, n_core)
        ]

    packets = pack(concept_ids, timesteps, txt_tokens[0], sizes, slice_width)
    packets = exchange(packets, CLASS)
    weights = by_core(kv_weight)
    bank, rstd = table_part(concept_table, by_core(mod_table), slice_width, n_core)
    terms = project(packets, bank, conc_dev, weights, sizes, head_dim, tok_len)
    terms = exchange(terms, CLASS)
    query, grad = img_query[0], out_grad[0]
    stats = image_part(query, img_key[0], img_value[0], grad, head_dim)
    packets = sample_part(
        concept_ids, positions, timesteps, terms, kv_bias.reshape(-1, head_dim), key_gain[None],
        stats, query, grad, sizes, tok_len, conc_dev, model_width,
    )
    packets = by_core(exchange(packets, CLASS))
    coef = rstd / counts.astype(F32)[:, None]
    return owner_part(packets, bank, n_core, coef, kv_weight)


def solution(mesh):
    n_dp, n_fsdp = mesh.shape["dp"], mesh.shape["fsdp"]
    n_core = 2 if n_fsdp % 2 == 0 else 1
    fine = Mesh(mesh.devices.reshape(n_dp, n_fsdp // n_core, n_core), ("dp", "chip", "core"))
    fsdp = ("chip", "core")
    every = ("dp",) + fsdp
    placed = (
        P(every, None, None),
        P("dp", None),
        P(every),
        P(every),
        P(every),
        P("dp"),
        P(None, None, fsdp),
        P(fsdp, None),
        P(),
        P(),
        P(every, None, None),
        P(every, None, None),
        P(every, None, None),
        P(every, None, None),
    )
    return jax.shard_map(
        shards, mesh=fine, in_specs=placed, out_specs=P("dp", fsdp), check_vma=False
    )
```

```python
import functools
import math

import jax
import jax.numpy as jnp
from jax import lax
from jax.experimental import pallas as pl
from jax.experimental.pallas import tpu as pltpu
from jax.sharding import Mesh, PartitionSpec as P

EPSILON = 1e-06
BF16 = jnp.bfloat16
F32 = jnp.float32
I32 = jnp.int32
LANES = 128
MIB = 1024 * 1024
SPARE_ROWS = 128
GRANT = dict(table=51.6, image=51.8, project=52.7, sample=51.8, owner=53.25)
NT = (((1,), (1,)), ((), ()))
TN = (((0,), (0,)), ((), ()))
EVERYONE = ("dp", "chip", "core")
CLASS = ("dp", "chip")


def dot(a, b):
    return jnp.dot(a, b, preferred_element_type=F32)


def dot_nt(a, b):
    return lax.dot_general(a, b, NT, preferred_element_type=F32)


def dot_tn(a, b):
    return lax.dot_general(a, b, TN, preferred_element_type=F32)


def split_bf16(x):
    high = x.astype(BF16)
    return high, (x - high.astype(F32)).astype(BF16)


def iota(shape, axis):
    return lax.broadcasted_iota(I32, shape, axis)


def hold(x):
    return ("hold", x)


def part(x, *cut):
    return ("part", x, cut)


def late_part(x, *cut):
    return ("late_part", x, cut)


def cut_shape(shape, cut):
    return tuple(c[1] for c in cut) + tuple(shape[len(cut) :])


def cut_index(cut):
    return tuple(pl.ds(*c) for c in cut)


def late(x, chunks, axis=1):
    return ("late", x, chunks, axis)


def scalar(x):
    return ("scalar", x)


def direct(x):
    return ("direct", x)


def call(body, operands, results, scratch=(), vmem=63, flops=2_000_000_000):
    arrays = [o[1] for o in operands]
    shapes = [jax.ShapeDtypeStruct(*r[:2]) for r in results]
    cuts = [r[2] if len(r) > 2 else () for r in results]
    n_in, n_out = len(arrays), len(shapes)
    counts = [o[2] if o[0] == "late" else 1 for o in operands]
    offsets = [sum(counts[:i]) for i in range(n_in)]
    n_sems = sum(counts) + n_out

    def kernel(*refs):
        ins, outs = refs[:n_in], refs[n_in : n_in + n_out]
        spare, made = refs[n_in + n_out : 2 * n_in + n_out], refs[2 * n_in + n_out : 2 * n_in + 2 * n_out]
        held = [r if o[0] in ("direct", "scalar") else h for o, r, h in zip(operands, ins, spare)]
        sems, extra = refs[2 * (n_in + n_out)], refs[2 * (n_in + n_out) + 1 :]

        def copies_of(i):
            o = operands[i]
            if o[0] in ("direct", "scalar"):
                return []
            if o[0] in ("part", "late_part"):
                return [pltpu.make_async_copy(ins[i].at[cut_index(o[2])], held[i], sems.at[offsets[i]])]
            if o[0] != "late" or o[2] == 1:
                return [pltpu.make_async_copy(ins[i], held[i], sems.at[offsets[i]])]
            size = o[1].shape[o[3]] // o[2]
            cut = lambda k: tuple([slice(None)] * o[3] + [pl.ds(k * size, size)])
            return [
                pltpu.make_async_copy(ins[i].at[cut(k)], held[i].at[cut(k)], sems.at[offsets[i] + k])
                for k in range(o[2])
            ]

        copies = [copies_of(i) for i in range(n_in)]
        is_late = [o[0] in ("late", "late_part") for o in operands]
        first = [c for i in range(n_in) if not is_late[i] for c in copies[i]]
        then = [i for i in range(n_in) if is_late[i]]
        for c in first:
            c.start()
        for k in range(max([counts[i] for i in then], default=0)):
            for i in then:
                if k < counts[i]:
                    copies[i][k].start()
        for c in first:
            c.wait()
        given = [
            (held[i], lambda k, i=i: copies[i][k].wait()) if is_late[i] else held[i]
            for i in range(n_in)
        ]
        body(given, made, extra)
        final = [
            pltpu.make_async_copy(m, out.at[cut_index(c)] if c else out, sems.at[sum(counts) + k])
            for k, (m, out, c) in enumerate(zip(made, outs, cuts))
        ]
        for c in final:
            c.start()
        for c in final:
            c.wait()

    def spare_of(o):
        shape = cut_shape(o[1].shape, o[2]) if o[0] in ("part", "late_part") else o[1].shape
        return pltpu.VMEM((8, LANES) if o[0] in ("direct", "scalar") else shape, o[1].dtype)

    spaces = {"direct": pltpu.VMEM, "scalar": pltpu.SMEM}
    return pl.pallas_call(
        kernel,
        in_specs=[
            pl.BlockSpec(memory_space=spaces.get(o[0], pltpu.HBM)) for o in operands
        ],
        out_specs=[pl.BlockSpec(memory_space=pltpu.HBM)] * n_out,
        out_shape=shapes,
        scratch_shapes=[spare_of(o) for o in operands]
        + [pltpu.VMEM(cut_shape(s.shape, c), s.dtype) for s, c in zip(shapes, cuts)]
        + [pltpu.SemaphoreType.DMA((n_sems,))]
        + list(scratch),
        compiler_params=pltpu.CompilerParams(vmem_limit_bytes=int(vmem * MIB)),
        cost_estimate=pl.CostEstimate(flops=flops, bytes_accessed=1024, transcendentals=0),
    )(*arrays)


def normalise(x):
    d = x - jnp.mean(x, -1, keepdims=True)
    rstd = lax.rsqrt(jnp.mean(d * d, -1, keepdims=True) + EPSILON)
    return d * rstd, rstd


SPECIAL = (2, 1, 1)


def slots_of(sizes, tok_len):
    return max(-(-(tok_len + sum(SPECIAL)) // sizes[0]), max(SPECIAL))


def special_at(step):
    return SPECIAL[step] if step < len(SPECIAL) else 0


def first_token(step, slots):
    passed = [slots * i - sum(SPECIAL[:i]) for i in range(len(SPECIAL) + 1)]
    far = passed[-1] + (step - len(SPECIAL)) * slots
    for i in range(len(SPECIAL)):
        far = jnp.where(step == i, passed[i], far)
    return far


def owner_of(concept, n_dp, conc_dev):
    owner = jnp.int32(0)
    for d in range(1, n_dp):
        owner += (concept >= d * conc_dev).astype(I32)
    return owner


def packet_rows(slots, n_core, width):
    need = -(-slots * n_core * width // LANES) + 1
    return need, -(-need // 8) * 8


def pack_body(sizes, width, slots, conc_dev, ins, outs, scratch):
    n_dp, n_chip, n_core = sizes
    ids, times, tokens = ins
    (out,), (held, chosen, flat) = outs, scratch
    tok_len = tokens.shape[0]
    need, rows = packet_rows(slots, n_core, width)
    pieces = width // LANES
    held[...] = normalise(tokens[...].astype(F32))[0]
    flat[...] = jnp.zeros(flat.shape, F32)
    lane = iota((1, LANES), 1)
    values = (ids[0] // 64, lax.rem(ids[0], 64), times[0])
    label = jnp.zeros((1, LANES), F32)
    for i, x in enumerate(values):
        label = jnp.where(lane == i, x.astype(F32), label)
    core = lax.axis_index("core")
    owner = owner_of(ids[0], n_dp, conc_dev)
    for d in range(n_dp):
        token = first_token(lax.rem(d + n_dp - owner, n_dp), slots)
        for i in range(slots):
            chosen[i : i + 1, :] = held[pl.ds(jnp.minimum(token + i, tok_len - 1), 1), :]
        for chip in range(n_chip):
            base = (d * n_chip + chip) * rows
            flat[base + need - 1 : base + need, :] = label
            for i in range(slots):
                for p in range(n_core):
                    at = (chip * n_core + (core ^ p)) * width
                    for k in range(pieces):
                        r = base + (i * n_core + p) * pieces + k
                        lanes = pl.ds(pl.multiple_of(at + k * LANES, LANES), LANES)
                        flat[r : r + 1, :] = chosen[i : i + 1, lanes]
    out[...] = flat[...].astype(BF16)


def hat_body(ins, outs, scratch):
    outs[0][...] = normalise(ins[0][...].astype(F32))[0].astype(BF16)


def pack(ids, times, tokens, sizes, width, conc_dev):
    n_dp, n_chip, n_core = sizes
    n_all = n_dp * n_chip
    tok_len, model_width = tokens.shape
    slots = slots_of(sizes, tok_len)
    need, rows = packet_rows(slots, n_core, width)
    if width % LANES == 0:
        (out,) = call(
            functools.partial(pack_body, sizes, width, slots, conc_dev),
            [scalar(ids), scalar(times), direct(tokens)],
            [((n_all * rows, LANES), BF16)],
            [
                pltpu.VMEM(tokens.shape, F32),
                pltpu.VMEM((-(-slots // 8) * 8, model_width), F32),
                pltpu.VMEM((n_all * rows, LANES), F32),
            ],
        )
        return out.reshape(n_all, rows, LANES)
    (hat,) = call(hat_body, [direct(tokens)], [(tokens.shape, BF16)])
    steps = (jnp.arange(n_dp, dtype=I32) + n_dp - owner_of(ids[0], n_dp, conc_dev)) % n_dp
    token = first_token(steps, slots)[:, None] + jnp.arange(slots, dtype=I32)[None, :]
    hat = jnp.take(hat, jnp.minimum(token, tok_len - 1).reshape(-1), axis=0)
    hat = hat.reshape(n_dp, slots, n_chip, n_core, width)
    core = lax.axis_index("core")
    own = [lax.dynamic_index_in_dim(hat, core ^ p, 3, keepdims=False) for p in range(n_core)]
    body = jnp.stack(own, 3).transpose(0, 2, 1, 3, 4).reshape(n_all, -1)
    body = jnp.pad(body, ((0, 0), (0, (need - 1) * LANES - body.shape[1])))
    label = jnp.stack([ids[0] // 64, ids[0] % 64, times[0]]).astype(BF16)
    label = jnp.broadcast_to(jnp.pad(label, (0, LANES - 3))[None], (n_all, LANES))
    out = jnp.concatenate([body, label], 1).reshape(n_all, need, LANES)
    return jnp.pad(out, ((0, 0), (0, rows - need), (0, 0)))


def bank_rows(conc_dev, buckets):
    return conc_dev + 2 * buckets


def table_body(width, n_core, ins, outs, scratch):
    (table, wait), mods, parts = ins[0], ins[1 : 1 + n_core], ins[1 + n_core :]
    bank, rstd_out = outs
    chip, core = lax.axis_index("chip"), lax.axis_index("core")
    rows, buckets = table.shape[0], mods[0].shape[0]
    each = bank_rows(rows, buckets)
    for p, mod in enumerate(mods):
        x = mod[...].astype(F32)
        for i in range(2):
            at = p * each + rows + i * buckets
            bank[at : at + buckets, :] = x[:, i, :].astype(BF16)
    block = rows // 2
    for i in range(2):
        wait(i)
        here = slice(i * block, (i + 1) * block)
        x = table[here, :].astype(F32)
        mean = jnp.mean(x, -1, keepdims=True)
        d = x - mean
        rstd = lax.rsqrt(jnp.mean(d * d, -1, keepdims=True) + EPSILON)
        rstd_out[here, :] = rstd
        for p in range(n_core):
            if parts:
                piece = parts[p][here, :]
            else:
                at = pl.multiple_of((chip * n_core + (core ^ p)) * width, LANES)
                piece = table[here, pl.ds(at, width)]
            to = slice(p * each + i * block, p * each + (i + 1) * block)
            bank[to, :] = ((piece.astype(F32) - mean) * rstd).astype(BF16)


def table_part(table, mods, width, n_core):
    rows = table.shape[0]
    buckets = mods[0].shape[0]
    parts = []
    if width % LANES:
        chip, core = lax.axis_index("chip"), lax.axis_index("core")
        cut = lambda p: lax.dynamic_slice_in_dim(table, (chip * n_core + (core ^ p)) * width, width, 1)
        parts = [hold(cut(p)) for p in range(n_core)]
    used = n_core * bank_rows(rows, buckets)
    return call(
        functools.partial(table_body, width, n_core),
        [late(table, 2, 0)] + [direct(m) for m in mods] + parts,
        [((used + SPARE_ROWS, width), BF16, ((0, used),)), ((rows, 1), F32)],
        vmem=GRANT["table"],
    )


def image_body(head_dim, chunks, ins, outs, scratch):
    (q, _), (k, _), (v, _), (g, _) = ins
    (out,) = outs
    scale = 1.0 / math.sqrt(head_dim)
    heads = out.shape[0]
    for h in range(heads):
        if h % (heads // chunks) == 0:
            for _, wait in ins:
                wait(h // (heads // chunks))
        cols = slice(h * head_dim, (h + 1) * head_dim)
        s = dot_nt(k[:, cols], q[:, cols]) * scale
        gv = dot_nt(v[:, cols], g[:, cols])
        top = jnp.max(s, 0, keepdims=True)
        e = jnp.exp(s - top)
        out[h, 0:1, :] = top
        out[h, 1:2, :] = jnp.sum(e, 0, keepdims=True)
        out[h, 2:3, :] = jnp.sum(e * gv, 0, keepdims=True)


def image_part(q, k, v, g, head_dim):
    rows, width = q.shape
    heads = width // head_dim
    chunks = math.gcd(heads, 2)
    (out,) = call(
        functools.partial(image_body, head_dim, chunks),
        [late(x, chunks) for x in (q, k, v, g)],
        [((heads, 8 + SPARE_ROWS, rows), F32, ((0, heads), (0, 8)))],
        vmem=GRANT["image"],
    )
    return out


def project_body(sizes, conc_dev, head_dim, slots, chunks, ins, outs, scratch):
    n_dp, n_chip, n_core = sizes
    n_all = n_dp * n_chip
    bank, weights, given = ins[0], ins[1 : 1 + n_core], ins[1 + n_core :]
    (out,), (lhs, flat, flat_in) = outs, scratch
    width, kv_width = weights[0][0].shape
    each = (bank.shape[0] - SPARE_ROWS) // n_core
    buckets = (each - conc_dev) // 2
    my_dp = lax.axis_index("dp")
    if len(given) == 1:
        need, rows = packet_rows(slots, n_core, width)
        pieces = width // LANES
        flat_in[...] = given[0][...].reshape(n_all * rows, LANES).astype(F32)
        row = lambda r: flat_in[pl.ds(r, n_all, stride=rows), :]
        labels = row(need - 1)
        token = lambda i, p: jnp.concatenate(
            [row((i * n_core + p) * pieces + k) for k in range(pieces)], 1
        )
    else:
        labels = given[1][...].astype(F32)
        token = lambda i, p: given[0][i, p].astype(F32)
    label = lambda i: labels[:, i : i + 1].astype(I32)
    ids, times = label(0) * 64 + label(1), label(2)
    pick_time = (iota((n_all, buckets), 1) == times).astype(BF16)
    pick_row = (iota((n_all, conc_dev), 1) == ids - my_dp * conc_dev).astype(BF16)

    def owned_by(step):
        first = lax.rem(my_dp + n_dp - step, n_dp) * conc_dev
        return (ids >= first) & (ids < first + conc_dev)

    for p in range(n_core):
        at = p * each + conc_dev
        shift = dot(pick_time, bank[at : at + buckets, :])
        scale = 1.0 + dot(pick_time, bank[at + buckets : at + 2 * buckets, :])
        conc = scale * dot(pick_row, bank[p * each : p * each + conc_dev, :]) + shift
        tokens = [scale * token(i, p) + shift for i in range(slots)]
        special = ([conc, jnp.zeros_like(conc)], [scale], [shift])
        for i in range(slots):
            value = tokens[i]
            for step, given_rows in enumerate(special):
                value = jnp.where(owned_by(step), (given_rows + tokens)[i], value)
            lhs[p, i * n_all : (i + 1) * n_all] = value.astype(BF16)
    owned = owned_by(0)
    kv_rows = kv_width // head_dim
    block = math.gcd(kv_width // chunks, 4 * head_dim)
    for at in range(0, kv_width, block):
        if at % (kv_width // chunks) == 0:
            for _, wait in weights:
                wait(at // (kv_width // chunks))
        cols = slice(at, at + block)
        terms = dot(lhs[0], weights[0][0][:, cols])
        for p in range(1, n_core):
            terms += dot(lhs[p], weights[p][0][:, cols])
        term = [terms[i * n_all : (i + 1) * n_all] for i in range(slots)]
        term[1] = jnp.where(owned, term[0] - term[0].astype(BF16).astype(F32), term[1])
        for i in range(slots):
            for r in range(block // head_dim):
                to = pl.ds(i * kv_rows + at // head_dim + r, n_all, stride=slots * kv_rows)
                flat[to, :] = term[i][:, r * head_dim : (r + 1) * head_dim]
    out[...] = flat[...].astype(BF16)


def project(packets, bank, conc_dev, weights, sizes, head_dim, tok_len):
    n_dp, n_chip, n_core = sizes
    width, kv_width = weights[0].shape
    slots = slots_of(sizes, tok_len)
    need, rows = packet_rows(slots, n_core, width)
    n_all = n_dp * n_chip
    kv_rows = kv_width // head_dim
    chunks = 3
    given = [direct(packets)]
    if width % LANES:
        body = packets[:, : need - 1].reshape(n_all, -1)[:, : slots * n_core * width]
        body = body.reshape(n_all, slots, n_core, width).transpose(1, 2, 0, 3)
        given = [hold(body), hold(packets[:, need - 1])]
    (out,) = call(
        functools.partial(project_body, sizes, conc_dev, head_dim, slots, chunks),
        [direct(bank)] + [late(w, chunks) for w in weights] + given,
        [((n_all * slots * kv_rows, head_dim), BF16)],
        [
            pltpu.VMEM((n_core, slots * n_all, width), BF16),
            pltpu.VMEM((n_all * slots * kv_rows, head_dim), F32),
            pltpu.VMEM((n_all * rows, LANES), F32),
        ],
        vmem=GRANT["project"],
    )
    return out.reshape(n_all, slots * kv_rows, head_dim)


def sample_body(sizes, tok_len, conc_dev, model_width, ins, outs, scratch):
    ids_ref, place_ref, time_ref, terms, bias, gain_ref, (stat_ref, stat_wait) = ins[:7]
    q, g = ins[7:]
    (out,), (toks,) = outs, scratch
    n_dp, n_chip, _ = sizes
    heads, _, img_len = stat_ref.shape
    kv_rows, head_dim = bias.shape
    scale = 1.0 / math.sqrt(head_dim)
    owner = owner_of(ids_ref[0], n_dp, conc_dev)
    slots = slots_of(sizes, tok_len)
    sums, t = [], 0
    for step in range(n_dp):
        first = lax.rem(owner + step, n_dp) * n_chip
        total = terms[first].astype(F32)
        for s in range(1, n_chip):
            total += terms[first + s].astype(F32)
        slot = lambda i: total[i * kv_rows : (i + 1) * kv_rows]
        sums += [slot(i) for i in range(special_at(step))]
        for i in range(special_at(step), slots):
            if t < tok_len:
                toks[t * kv_rows : (t + 1) * kv_rows, :] = slot(i)
                t += 1
    conc, scale_sum, shift_sum = sums[0] + sums[1], sums[2], sums[3]
    full = conc + bias[...]
    raw_pos = full[:heads]
    inv_pos = lax.rsqrt(jnp.mean(raw_pos * raw_pos, -1, keepdims=True) + EPSILON)
    gain = gain_ref[...]
    at_pos = iota((tok_len, 1), 0) == place_ref[0]

    def text_rows(r):
        part = toks[pl.ds(r, tok_len, stride=kv_rows), :] + bias[r : r + 1, :]
        return jnp.where(at_pos, full[r : r + 1], part)

    keys, vals = [], []
    for h in range(heads):
        raw = text_rows(h)
        inv = lax.rsqrt(jnp.mean(raw * raw, -1, keepdims=True) + EPSILON)
        keys.append((raw * inv * gain).astype(BF16))
        vals.append(text_rows(heads + h).astype(BF16))
    cols = lambda h: slice(h * head_dim, (h + 1) * head_dim)
    shape = (heads, tok_len, img_len)
    s = jnp.concatenate([dot_nt(keys[h], q[:, cols(h)]) for h in range(heads)], 0)
    gv = jnp.concatenate([dot_nt(vals[h], g[:, cols(h)]) for h in range(heads)], 0)
    s, gv = s.reshape(shape) * scale, gv.reshape(shape)
    stat_wait(0)
    stats = stat_ref[...]
    top, total, weighted = stats[:, 0:1, :], stats[:, 1:2, :], stats[:, 2:3, :]
    new_top = jnp.maximum(top, jnp.max(s, 1, keepdims=True))
    e = jnp.exp(s - new_top)
    keep = jnp.exp(top - new_top)
    inv_total = 1.0 / (total * keep + jnp.sum(e, 1, keepdims=True))
    delta = (weighted * keep + jnp.sum(e * gv, 1, keepdims=True)) * inv_total
    here = iota((1, tok_len, 1), 1) == place_ref[0]
    p = jnp.sum(jnp.where(here, e, 0.0), 1, keepdims=True) * inv_total
    dscore = p * (jnp.sum(jnp.where(here, gv, 0.0), 1, keepdims=True) - delta)
    row = iota((1, 8, 1), 1)

    def two_rows(x):
        high = x.astype(BF16).astype(F32)
        return jnp.where(row == 0, high, jnp.where(row == 1, x - high, 0.0)).astype(BF16)

    p2, d2 = two_rows(p), two_rows(dscore)
    val_rows = [jnp.sum(dot(p2[h], g[:, cols(h)]), 0, keepdims=True) for h in range(heads)]
    key_rows = [jnp.sum(dot(d2[h], q[:, cols(h)]), 0, keepdims=True) for h in range(heads)]
    dn = jnp.concatenate(key_rows, 0) * scale * gain
    normed = raw_pos * inv_pos
    draw = inv_pos * (dn - normed * jnp.mean(dn * normed, -1, keepdims=True))
    dkv = jnp.concatenate([draw] + val_rows, 0)

    def total_of(x):
        return jnp.sum(jnp.sum(x, 0, keepdims=True), 1, keepdims=True) * (1.0 / model_width)

    means = split_bf16(total_of(dkv * scale_sum)) + split_bf16(total_of(dkv * (conc - shift_sum)))
    labels = (ids_ref[0] // 64, lax.rem(ids_ref[0], 64), time_ref[0])
    lane = iota((8, head_dim), 1)
    side = jnp.zeros((8, head_dim), F32)
    for i, x in enumerate(means + labels):
        side = jnp.where(lane == i, x.astype(F32), side)
    packet = jnp.concatenate([dkv, side], 0).astype(BF16)
    out[...] = jnp.broadcast_to(packet[None], out.shape)


def sample_part(ids, places, times, terms, bias, gain, stats, q, g, sizes, tok_len, conc_dev, model_width):
    kv_rows, head_dim = bias.shape
    (out,) = call(
        functools.partial(sample_body, sizes, tok_len, conc_dev, model_width),
        [scalar(ids), scalar(places), scalar(times), direct(terms), direct(bias), direct(gain)]
        + [late_part(stats, (0, stats.shape[0]), (0, 8))]
        + [direct(q), direct(g)],
        [((sizes[0] * sizes[1], kv_rows + 8, head_dim), BF16)],
        [
            pltpu.VMEM((tok_len * kv_rows, head_dim), F32),
        ],
        vmem=GRANT["sample"],
    )
    return out


def owner_body(chunks, ins, outs, scratch):
    (bank, bank_wait), (coef, coef_wait), (weight, wait), packets = *ins[:3], ins[3:]
    (out,), (flat,) = outs, scratch
    n_each, rows, head_dim = packets[0].shape
    n_dev = n_each * len(packets)
    conc_dev = coef.shape[0]
    buckets = (bank.shape[0] - conc_dev) // 2
    parts = weight.shape[1] // head_dim
    first = lax.axis_index("dp") * conc_dev
    for i, x in enumerate(packets):
        flat[i * n_each * rows : (i + 1) * n_each * rows, :] = (
            x[...].reshape(n_each * rows, head_dim).astype(F32)
        )
    piece = lambda r: flat[pl.ds(r, n_dev, stride=rows), :]
    side = piece(parts)
    column = lambda i: side[:, i : i + 1]
    mean_1, mean_2 = column(0) + column(1), column(2) + column(3)
    side_rows = side.T
    row = lambda i: side_rows[i : i + 1, :].astype(I32)
    ids_row = row(4) * 64 + row(5) - first
    owned = (iota((conc_dev, n_dev), 0) == ids_row).astype(BF16)
    owned = jnp.concatenate([owned, owned], 1)
    mine = column(4).astype(I32) * 64 + column(5).astype(I32) - first
    times = column(6).astype(I32)
    bank_wait(0)
    scale = 1.0 + dot((iota((n_dev, buckets), 1) == times).astype(BF16), bank[conc_dev + buckets :, :])
    one_hot = (iota((n_dev, conc_dev), 1) == mine).astype(BF16)
    offset = mean_1 + dot(one_hot, bank[0:conc_dev, :]) * mean_2
    coef_wait(0)
    factor = jnp.broadcast_to(coef[...], out.shape)
    size = parts // chunks
    grad = jnp.zeros((n_dev, weight.shape[0]), F32)
    for i in range(chunks):
        dkv = jnp.concatenate([piece(r).astype(BF16) for r in range(i * size, (i + 1) * size)], 1)
        wait(i)
        grad += dot_nt(dkv, weight[:, i * size * head_dim : (i + 1) * size * head_dim])
    high, low = split_bf16(grad * scale - offset)
    out[...] = dot(owned, jnp.concatenate([high, low], 0)) * factor


def owner_part(packets, bank, n_core, coef, weight):
    each = (bank.shape[0] - SPARE_ROWS) // n_core
    n_each, rows, head_dim = packets[0].shape
    n_dev = n_each * len(packets)
    (out,) = call(
        functools.partial(owner_body, 3),
        [late_part(bank, (0, each)), late(coef, 1), late(weight, 3)] + [direct(x) for x in packets],
        [((coef.shape[0], weight.shape[0]), F32)],
        [pltpu.VMEM((n_dev * rows, head_dim), F32)],
        vmem=GRANT["owner"],
    )
    return out


def exchange(x, axes):
    return lax.all_to_all(x, axes, 0, 0, tiled=True)


def shards(
    txt_tokens,
    concept_table,
    concept_ids,
    positions,
    timesteps,
    counts,
    mod_table,
    kv_weight,
    kv_bias,
    key_gain,
    img_query,
    img_key,
    img_value,
    out_grad,
):
    sizes = tuple(lax.axis_size(a) for a in EVERYONE)
    n_dp, n_chip, n_core = sizes
    _, tok_len, model_width = txt_tokens.shape
    slice_width = kv_weight.shape[0]
    head_dim = key_gain.shape[0]
    conc_dev = concept_table.shape[0]

    def by_core(x):
        return [x] + [
            lax.ppermute(x, "core", [(i, i ^ s) for i in range(n_core)]) for s in range(1, n_core)
        ]

    packets = pack(concept_ids, timesteps, txt_tokens[0], sizes, slice_width, conc_dev)
    packets = exchange(packets, CLASS)
    weights = by_core(kv_weight)
    bank, rstd = table_part(concept_table, by_core(mod_table), slice_width, n_core)
    terms = project(packets, bank, conc_dev, weights, sizes, head_dim, tok_len)
    terms = exchange(terms, CLASS)
    query, grad = img_query[0], out_grad[0]
    stats = image_part(query, img_key[0], img_value[0], grad, head_dim)
    packets = sample_part(
        concept_ids, positions, timesteps, terms, kv_bias.reshape(-1, head_dim), key_gain[None],
        stats, query, grad, sizes, tok_len, conc_dev, model_width,
    )
    packets = by_core(exchange(packets, CLASS))
    coef = rstd / counts.astype(F32)[:, None]
    return owner_part(packets, bank, n_core, coef, kv_weight)


def solution(mesh):
    n_dp, n_fsdp = mesh.shape["dp"], mesh.shape["fsdp"]
    n_core = 2 if n_fsdp % 2 == 0 else 1
    fine = Mesh(mesh.devices.reshape(n_dp, n_fsdp // n_core, n_core), ("dp", "chip", "core"))
    fsdp = ("chip", "core")
    every = ("dp",) + fsdp
    placed = (
        P(every, None, None),
        P("dp", None),
        P(every),
        P(every),
        P(every),
        P("dp"),
        P(None, None, fsdp),
        P(fsdp, None),
        P(),
        P(),
        P(every, None, None),
        P(every, None, None),
        P(every, None, None),
        P(every, None, None),
    )
    return jax.shard_map(
        shards, mesh=fine, in_specs=placed, out_specs=P("dp", fsdp), check_vma=False
    )
```

```python
import functools
import math

import jax
import jax.numpy as jnp
from jax import lax
from jax.experimental import pallas as pl
from jax.experimental.pallas import tpu as pltpu
from jax.sharding import Mesh, PartitionSpec as P

EPSILON = 1e-06
BF16 = jnp.bfloat16
F32 = jnp.float32
I32 = jnp.int32
LANES = 128
MIB = 1024 * 1024
SPARE_ROWS = 128
GRANT = dict(table=51.6, image=51.8, project=52.7, sample=51.8, owner=53.25)
NT = (((1,), (1,)), ((), ()))
TN = (((0,), (0,)), ((), ()))
EVERYONE = ("dp", "chip", "core")
CLASS = ("dp", "chip")


def dot(a, b):
    return jnp.dot(a, b, preferred_element_type=F32)


def dot_nt(a, b):
    return lax.dot_general(a, b, NT, preferred_element_type=F32)


def dot_tn(a, b):
    return lax.dot_general(a, b, TN, preferred_element_type=F32)


def split_bf16(x):
    high = x.astype(BF16)
    return high, (x - high.astype(F32)).astype(BF16)


def iota(shape, axis):
    return lax.broadcasted_iota(I32, shape, axis)


def hold(x):
    return ("hold", x)


def part(x, *cut):
    return ("part", x, cut)


def late_part(x, *cut):
    return ("late_part", x, cut)


def cut_shape(shape, cut):
    return tuple(c[1] for c in cut) + tuple(shape[len(cut) :])


def cut_index(cut):
    return tuple(pl.ds(*c) for c in cut)


def late(x, chunks, axis=1):
    return ("late", x, chunks, axis)


def scalar(x):
    return ("scalar", x)


def direct(x):
    return ("direct", x)


def call(body, operands, results, scratch=(), vmem=63, flops=2_000_000_000):
    arrays = [o[1] for o in operands]
    shapes = [jax.ShapeDtypeStruct(*r[:2]) for r in results]
    cuts = [r[2] if len(r) > 2 else () for r in results]
    n_in, n_out = len(arrays), len(shapes)
    counts = [o[2] if o[0] == "late" else 1 for o in operands]
    offsets = [sum(counts[:i]) for i in range(n_in)]
    n_sems = sum(counts) + n_out

    def kernel(*refs):
        ins, outs = refs[:n_in], refs[n_in : n_in + n_out]
        spare, made = refs[n_in + n_out : 2 * n_in + n_out], refs[2 * n_in + n_out : 2 * n_in + 2 * n_out]
        held = [r if o[0] in ("direct", "scalar") else h for o, r, h in zip(operands, ins, spare)]
        sems, extra = refs[2 * (n_in + n_out)], refs[2 * (n_in + n_out) + 1 :]

        def copies_of(i):
            o = operands[i]
            if o[0] in ("direct", "scalar"):
                return []
            if o[0] in ("part", "late_part"):
                return [pltpu.make_async_copy(ins[i].at[cut_index(o[2])], held[i], sems.at[offsets[i]])]
            if o[0] != "late" or o[2] == 1:
                return [pltpu.make_async_copy(ins[i], held[i], sems.at[offsets[i]])]
            size = o[1].shape[o[3]] // o[2]
            cut = lambda k: tuple([slice(None)] * o[3] + [pl.ds(k * size, size)])
            return [
                pltpu.make_async_copy(ins[i].at[cut(k)], held[i].at[cut(k)], sems.at[offsets[i] + k])
                for k in range(o[2])
            ]

        copies = [copies_of(i) for i in range(n_in)]
        is_late = [o[0] in ("late", "late_part") for o in operands]
        first = [c for i in range(n_in) if not is_late[i] for c in copies[i]]
        then = [i for i in range(n_in) if is_late[i]]
        for c in first:
            c.start()
        for k in range(max([counts[i] for i in then], default=0)):
            for i in then:
                if k < counts[i]:
                    copies[i][k].start()
        for c in first:
            c.wait()
        given = [
            (held[i], lambda k, i=i: copies[i][k].wait()) if is_late[i] else held[i]
            for i in range(n_in)
        ]
        body(given, made, extra)
        final = [
            pltpu.make_async_copy(m, out.at[cut_index(c)] if c else out, sems.at[sum(counts) + k])
            for k, (m, out, c) in enumerate(zip(made, outs, cuts))
        ]
        for c in final:
            c.start()
        for c in final:
            c.wait()

    def spare_of(o):
        shape = cut_shape(o[1].shape, o[2]) if o[0] in ("part", "late_part") else o[1].shape
        return pltpu.VMEM((8, LANES) if o[0] in ("direct", "scalar") else shape, o[1].dtype)

    spaces = {"direct": pltpu.VMEM, "scalar": pltpu.SMEM}
    return pl.pallas_call(
        kernel,
        in_specs=[
            pl.BlockSpec(memory_space=spaces.get(o[0], pltpu.HBM)) for o in operands
        ],
        out_specs=[pl.BlockSpec(memory_space=pltpu.HBM)] * n_out,
        out_shape=shapes,
        scratch_shapes=[spare_of(o) for o in operands]
        + [pltpu.VMEM(cut_shape(s.shape, c), s.dtype) for s, c in zip(shapes, cuts)]
        + [pltpu.SemaphoreType.DMA((n_sems,))]
        + list(scratch),
        compiler_params=pltpu.CompilerParams(vmem_limit_bytes=int(vmem * MIB)),
        cost_estimate=pl.CostEstimate(flops=flops, bytes_accessed=1024, transcendentals=0),
    )(*arrays)


def normalise(x):
    d = x - jnp.mean(x, -1, keepdims=True)
    rstd = lax.rsqrt(jnp.mean(d * d, -1, keepdims=True) + EPSILON)
    return d * rstd, rstd


SPECIAL = (2, 1, 1)


def slots_of(sizes, tok_len):
    return max(-(-(tok_len + sum(SPECIAL)) // sizes[0]), max(SPECIAL))


def special_at(step):
    return SPECIAL[step] if step < len(SPECIAL) else 0


def first_token(step, slots):
    passed = [slots * i - sum(SPECIAL[:i]) for i in range(len(SPECIAL) + 1)]
    far = passed[-1] + (step - len(SPECIAL)) * slots
    for i in range(len(SPECIAL)):
        far = jnp.where(step == i, passed[i], far)
    return far


def owner_of(concept, n_dp, conc_dev):
    owner = jnp.int32(0)
    for d in range(1, n_dp):
        owner += (concept >= d * conc_dev).astype(I32)
    return owner


def packet_rows(slots, n_core, width):
    need = -(-slots * n_core * width // LANES) + 1
    return need, -(-need // 8) * 8


def pack_body(sizes, width, slots, conc_dev, ins, outs, scratch):
    n_dp, n_chip, n_core = sizes
    ids, times, tokens = ins
    (out,), (held, flat) = outs, scratch
    tok_len = tokens.shape[0]
    need, rows = packet_rows(slots, n_core, width)
    pieces = width // LANES
    held[...] = normalise(tokens[...].astype(F32))[0]
    flat[...] = jnp.zeros(flat.shape, F32)
    lane = iota((1, LANES), 1)
    values = (ids[0] // 64, lax.rem(ids[0], 64), times[0])
    label = jnp.zeros((1, LANES), F32)
    for i, x in enumerate(values):
        label = jnp.where(lane == i, x.astype(F32), label)
    core = lax.axis_index("core")
    owner = owner_of(ids[0], n_dp, conc_dev)
    token = 0
    for step in range(n_dp):
        d = lax.rem(owner + step, n_dp)
        count = min(slots - special_at(step), tok_len - token)
        for chip in range(n_chip):
            to = d * n_chip + chip
            flat[to, need - 1 : need, :] = label
            for i in range(count):
                for p in range(n_core):
                    at = (chip * n_core + (core ^ p)) * width
                    for k in range(pieces):
                        r = (i * n_core + p) * pieces + k
                        lanes = pl.ds(pl.multiple_of(at + k * LANES, LANES), LANES)
                        flat[to, r : r + 1, :] = held[token + i : token + i + 1, lanes]
        token += count
    out[...] = flat[...].reshape(out.shape).astype(BF16)


def hat_body(ins, outs, scratch):
    outs[0][...] = normalise(ins[0][...].astype(F32))[0].astype(BF16)


def pack(ids, times, tokens, sizes, width, conc_dev):
    n_dp, n_chip, n_core = sizes
    n_all = n_dp * n_chip
    tok_len, model_width = tokens.shape
    slots = slots_of(sizes, tok_len)
    need, rows = packet_rows(slots, n_core, width)
    if width % LANES == 0:
        (out,) = call(
            functools.partial(pack_body, sizes, width, slots, conc_dev),
            [scalar(ids), scalar(times), direct(tokens)],
            [((n_all * rows, LANES), BF16)],
            [
                pltpu.VMEM(tokens.shape, F32),
                pltpu.VMEM((n_all, rows, LANES), F32),
            ],
        )
        return out.reshape(n_all, rows, LANES)
    (hat,) = call(hat_body, [direct(tokens)], [(tokens.shape, BF16)])
    steps = (jnp.arange(n_dp, dtype=I32) + n_dp - owner_of(ids[0], n_dp, conc_dev)) % n_dp
    token = first_token(steps, slots)[:, None] + jnp.arange(slots, dtype=I32)[None, :]
    hat = jnp.take(hat, jnp.minimum(token, tok_len - 1).reshape(-1), axis=0)
    hat = hat.reshape(n_dp, slots, n_chip, n_core, width)
    core = lax.axis_index("core")
    own = [lax.dynamic_index_in_dim(hat, core ^ p, 3, keepdims=False) for p in range(n_core)]
    body = jnp.stack(own, 3).transpose(0, 2, 1, 3, 4).reshape(n_all, -1)
    body = jnp.pad(body, ((0, 0), (0, (need - 1) * LANES - body.shape[1])))
    label = jnp.stack([ids[0] // 64, ids[0] % 64, times[0]]).astype(BF16)
    label = jnp.broadcast_to(jnp.pad(label, (0, LANES - 3))[None], (n_all, LANES))
    out = jnp.concatenate([body, label], 1).reshape(n_all, need, LANES)
    return jnp.pad(out, ((0, 0), (0, rows - need), (0, 0)))


def bank_rows(conc_dev, buckets):
    return conc_dev + 2 * buckets


def table_body(width, n_core, ins, outs, scratch):
    (table, wait), mods, parts = ins[0], ins[1 : 1 + n_core], ins[1 + n_core :]
    bank, rstd_out = outs
    chip, core = lax.axis_index("chip"), lax.axis_index("core")
    rows, buckets = table.shape[0], mods[0].shape[0]
    each = bank_rows(rows, buckets)
    for p, mod in enumerate(mods):
        x = mod[...].astype(F32)
        for i in range(2):
            at = p * each + rows + i * buckets
            bank[at : at + buckets, :] = x[:, i, :].astype(BF16)
    block = rows // 2
    for i in range(2):
        wait(i)
        here = slice(i * block, (i + 1) * block)
        x = table[here, :].astype(F32)
        mean = jnp.mean(x, -1, keepdims=True)
        d = x - mean
        rstd = lax.rsqrt(jnp.mean(d * d, -1, keepdims=True) + EPSILON)
        rstd_out[here, :] = rstd
        for p in range(n_core):
            if parts:
                piece = parts[p][here, :]
            else:
                at = pl.multiple_of((chip * n_core + (core ^ p)) * width, LANES)
                piece = table[here, pl.ds(at, width)]
            to = slice(p * each + i * block, p * each + (i + 1) * block)
            bank[to, :] = ((piece.astype(F32) - mean) * rstd).astype(BF16)


def table_part(table, mods, width, n_core):
    rows = table.shape[0]
    buckets = mods[0].shape[0]
    parts = []
    if width % LANES:
        chip, core = lax.axis_index("chip"), lax.axis_index("core")
        cut = lambda p: lax.dynamic_slice_in_dim(table, (chip * n_core + (core ^ p)) * width, width, 1)
        parts = [hold(cut(p)) for p in range(n_core)]
    used = n_core * bank_rows(rows, buckets)
    return call(
        functools.partial(table_body, width, n_core),
        [late(table, 2, 0)] + [direct(m) for m in mods] + parts,
        [((used + SPARE_ROWS, width), BF16, ((0, used),)), ((rows, 1), F32)],
        vmem=GRANT["table"],
    )


def image_body(head_dim, chunks, ins, outs, scratch):
    (q, _), (k, _), (v, _), (g, _) = ins
    (out,) = outs
    scale = 1.0 / math.sqrt(head_dim)
    heads = out.shape[0]
    for h in range(heads):
        if h % (heads // chunks) == 0:
            for _, wait in ins:
                wait(h // (heads // chunks))
        cols = slice(h * head_dim, (h + 1) * head_dim)
        s = dot_nt(k[:, cols], q[:, cols]) * scale
        gv = dot_nt(v[:, cols], g[:, cols])
        top = jnp.max(s, 0, keepdims=True)
        e = jnp.exp(s - top)
        out[h, 0:1, :] = top
        out[h, 1:2, :] = jnp.sum(e, 0, keepdims=True)
        out[h, 2:3, :] = jnp.sum(e * gv, 0, keepdims=True)


def image_part(q, k, v, g, head_dim):
    rows, width = q.shape
    heads = width // head_dim
    chunks = math.gcd(heads, 2)
    (out,) = call(
        functools.partial(image_body, head_dim, chunks),
        [late(x, chunks) for x in (q, k, v, g)],
        [((heads, 8 + SPARE_ROWS, rows), F32, ((0, heads), (0, 8)))],
        vmem=GRANT["image"],
    )
    return out


def project_body(sizes, conc_dev, head_dim, slots, chunks, ins, outs, scratch):
    n_dp, n_chip, n_core = sizes
    n_all = n_dp * n_chip
    bank, weights, given = ins[0], ins[1 : 1 + n_core], ins[1 + n_core :]
    (out,), (lhs, flat, flat_in) = outs, scratch
    width, kv_width = weights[0][0].shape
    each = (bank.shape[0] - SPARE_ROWS) // n_core
    buckets = (each - conc_dev) // 2
    my_dp = lax.axis_index("dp")
    if len(given) == 1:
        need, rows = packet_rows(slots, n_core, width)
        pieces = width // LANES
        flat_in[...] = given[0][...].reshape(n_all * rows, LANES).astype(F32)
        row = lambda r: flat_in[pl.ds(r, n_all, stride=rows), :]
        labels = row(need - 1)
        token = lambda i, p: jnp.concatenate(
            [row((i * n_core + p) * pieces + k) for k in range(pieces)], 1
        )
    else:
        labels = given[1][...].astype(F32)
        token = lambda i, p: given[0][i, p].astype(F32)
    label = lambda i: labels[:, i : i + 1].astype(I32)
    ids, times = label(0) * 64 + label(1), label(2)
    pick_time = (iota((n_all, buckets), 1) == times).astype(BF16)
    pick_row = (iota((n_all, conc_dev), 1) == ids - my_dp * conc_dev).astype(BF16)

    def owned_by(step):
        first = lax.rem(my_dp + n_dp - step, n_dp) * conc_dev
        return (ids >= first) & (ids < first + conc_dev)

    for p in range(n_core):
        at = p * each + conc_dev
        shift = dot(pick_time, bank[at : at + buckets, :])
        scale = 1.0 + dot(pick_time, bank[at + buckets : at + 2 * buckets, :])
        conc = scale * dot(pick_row, bank[p * each : p * each + conc_dev, :]) + shift
        tokens = [scale * token(i, p) + shift for i in range(slots)]
        special = ([conc, jnp.zeros_like(conc)], [scale], [shift])
        for i in range(slots):
            value = tokens[i]
            for step, given_rows in enumerate(special):
                value = jnp.where(owned_by(step), (given_rows + tokens)[i], value)
            lhs[p, i * n_all : (i + 1) * n_all] = value.astype(BF16)
    owned = owned_by(0)
    kv_rows = kv_width // head_dim
    block = math.gcd(kv_width // chunks, 4 * head_dim)
    for at in range(0, kv_width, block):
        if at % (kv_width // chunks) == 0:
            for _, wait in weights:
                wait(at // (kv_width // chunks))
        cols = slice(at, at + block)
        terms = dot(lhs[0], weights[0][0][:, cols])
        for p in range(1, n_core):
            terms += dot(lhs[p], weights[p][0][:, cols])
        term = [terms[i * n_all : (i + 1) * n_all] for i in range(slots)]
        term[1] = jnp.where(owned, term[0] - term[0].astype(BF16).astype(F32), term[1])
        for i in range(slots):
            for r in range(block // head_dim):
                to = pl.ds(i * kv_rows + at // head_dim + r, n_all, stride=slots * kv_rows)
                flat[to, :] = term[i][:, r * head_dim : (r + 1) * head_dim]
    out[...] = flat[...].astype(BF16)


def project(packets, bank, conc_dev, weights, sizes, head_dim, tok_len):
    n_dp, n_chip, n_core = sizes
    width, kv_width = weights[0].shape
    slots = slots_of(sizes, tok_len)
    need, rows = packet_rows(slots, n_core, width)
    n_all = n_dp * n_chip
    kv_rows = kv_width // head_dim
    chunks = 3
    given = [direct(packets)]
    if width % LANES:
        body = packets[:, : need - 1].reshape(n_all, -1)[:, : slots * n_core * width]
        body = body.reshape(n_all, slots, n_core, width).transpose(1, 2, 0, 3)
        given = [hold(body), hold(packets[:, need - 1])]
    (out,) = call(
        functools.partial(project_body, sizes, conc_dev, head_dim, slots, chunks),
        [direct(bank)] + [late(w, chunks) for w in weights] + given,
        [((n_all * slots * kv_rows, head_dim), BF16)],
        [
            pltpu.VMEM((n_core, slots * n_all, width), BF16),
            pltpu.VMEM((n_all * slots * kv_rows, head_dim), F32),
            pltpu.VMEM((n_all * rows, LANES), F32),
        ],
        vmem=GRANT["project"],
    )
    return out.reshape(n_all, slots * kv_rows, head_dim)


def sample_body(sizes, tok_len, conc_dev, model_width, ins, outs, scratch):
    ids_ref, place_ref, time_ref, terms, bias, gain_ref, (stat_ref, stat_wait) = ins[:7]
    q, g = ins[7:]
    (out,), (toks,) = outs, scratch
    n_dp, n_chip, _ = sizes
    heads, _, img_len = stat_ref.shape
    kv_rows, head_dim = bias.shape
    scale = 1.0 / math.sqrt(head_dim)
    owner = owner_of(ids_ref[0], n_dp, conc_dev)
    slots = slots_of(sizes, tok_len)
    sums, t = [], 0
    for step in range(n_dp):
        first = lax.rem(owner + step, n_dp) * n_chip
        total = terms[first].astype(F32)
        for s in range(1, n_chip):
            total += terms[first + s].astype(F32)
        slot = lambda i: total[i * kv_rows : (i + 1) * kv_rows]
        sums += [slot(i) for i in range(special_at(step))]
        for i in range(special_at(step), slots):
            if t < tok_len:
                toks[t * kv_rows : (t + 1) * kv_rows, :] = slot(i)
                t += 1
    conc, scale_sum, shift_sum = sums[0] + sums[1], sums[2], sums[3]
    full = conc + bias[...]
    raw_pos = full[:heads]
    inv_pos = lax.rsqrt(jnp.mean(raw_pos * raw_pos, -1, keepdims=True) + EPSILON)
    gain = gain_ref[...]
    at_pos = iota((tok_len, 1), 0) == place_ref[0]

    def text_rows(r):
        part = toks[pl.ds(r, tok_len, stride=kv_rows), :] + bias[r : r + 1, :]
        return jnp.where(at_pos, full[r : r + 1], part)

    keys, vals = [], []
    for h in range(heads):
        raw = text_rows(h)
        inv = lax.rsqrt(jnp.mean(raw * raw, -1, keepdims=True) + EPSILON)
        keys.append((raw * inv * gain).astype(BF16))
        vals.append(text_rows(heads + h).astype(BF16))
    cols = lambda h: slice(h * head_dim, (h + 1) * head_dim)
    shape = (heads, tok_len, img_len)
    s = jnp.concatenate([dot_nt(keys[h], q[:, cols(h)]) for h in range(heads)], 0)
    gv = jnp.concatenate([dot_nt(vals[h], g[:, cols(h)]) for h in range(heads)], 0)
    s, gv = s.reshape(shape) * scale, gv.reshape(shape)
    stat_wait(0)
    stats = stat_ref[...]
    top, total, weighted = stats[:, 0:1, :], stats[:, 1:2, :], stats[:, 2:3, :]
    new_top = jnp.maximum(top, jnp.max(s, 1, keepdims=True))
    e = jnp.exp(s - new_top)
    keep = jnp.exp(top - new_top)
    inv_total = 1.0 / (total * keep + jnp.sum(e, 1, keepdims=True))
    delta = (weighted * keep + jnp.sum(e * gv, 1, keepdims=True)) * inv_total
    here = iota((1, tok_len, 1), 1) == place_ref[0]
    p = jnp.sum(jnp.where(here, e, 0.0), 1, keepdims=True) * inv_total
    dscore = p * (jnp.sum(jnp.where(here, gv, 0.0), 1, keepdims=True) - delta)
    row = iota((1, 8, 1), 1)

    def two_rows(x):
        high = x.astype(BF16).astype(F32)
        return jnp.where(row == 0, high, jnp.where(row == 1, x - high, 0.0)).astype(BF16)

    p2, d2 = two_rows(p), two_rows(dscore)
    val_rows = [jnp.sum(dot(p2[h], g[:, cols(h)]), 0, keepdims=True) for h in range(heads)]
    key_rows = [jnp.sum(dot(d2[h], q[:, cols(h)]), 0, keepdims=True) for h in range(heads)]
    dn = jnp.concatenate(key_rows, 0) * scale * gain
    normed = raw_pos * inv_pos
    draw = inv_pos * (dn - normed * jnp.mean(dn * normed, -1, keepdims=True))
    dkv = jnp.concatenate([draw] + val_rows, 0)

    def total_of(x):
        return jnp.sum(jnp.sum(x, 0, keepdims=True), 1, keepdims=True) * (1.0 / model_width)

    means = split_bf16(total_of(dkv * scale_sum)) + split_bf16(total_of(dkv * (conc - shift_sum)))
    labels = (ids_ref[0] // 64, lax.rem(ids_ref[0], 64), time_ref[0])
    lane = iota((8, head_dim), 1)
    side = jnp.zeros((8, head_dim), F32)
    for i, x in enumerate(means + labels):
        side = jnp.where(lane == i, x.astype(F32), side)
    packet = jnp.concatenate([dkv, side], 0).astype(BF16)
    out[...] = jnp.broadcast_to(packet[None], out.shape)


def sample_part(ids, places, times, terms, bias, gain, stats, q, g, sizes, tok_len, conc_dev, model_width):
    kv_rows, head_dim = bias.shape
    (out,) = call(
        functools.partial(sample_body, sizes, tok_len, conc_dev, model_width),
        [scalar(ids), scalar(places), scalar(times), direct(terms), direct(bias), direct(gain)]
        + [late_part(stats, (0, stats.shape[0]), (0, 8))]
        + [direct(q), direct(g)],
        [((sizes[0] * sizes[1], kv_rows + 8, head_dim), BF16)],
        [
            pltpu.VMEM((tok_len * kv_rows, head_dim), F32),
        ],
        vmem=GRANT["sample"],
    )
    return out


def owner_body(chunks, ins, outs, scratch):
    (bank, bank_wait), (coef, coef_wait), (weight, wait), packets = *ins[:3], ins[3:]
    (out,), (flat,) = outs, scratch
    n_each, rows, head_dim = packets[0].shape
    n_dev = n_each * len(packets)
    conc_dev = coef.shape[0]
    buckets = (bank.shape[0] - conc_dev) // 2
    parts = weight.shape[1] // head_dim
    first = lax.axis_index("dp") * conc_dev
    for i, x in enumerate(packets):
        flat[i * n_each * rows : (i + 1) * n_each * rows, :] = (
            x[...].reshape(n_each * rows, head_dim).astype(F32)
        )
    piece = lambda r: flat[pl.ds(r, n_dev, stride=rows), :]
    side = piece(parts)
    column = lambda i: side[:, i : i + 1]
    mean_1, mean_2 = column(0) + column(1), column(2) + column(3)
    side_rows = side.T
    row = lambda i: side_rows[i : i + 1, :].astype(I32)
    ids_row = row(4) * 64 + row(5) - first
    owned = (iota((conc_dev, n_dev), 0) == ids_row).astype(BF16)
    owned = jnp.concatenate([owned, owned], 1)
    mine = column(4).astype(I32) * 64 + column(5).astype(I32) - first
    times = column(6).astype(I32)
    bank_wait(0)
    scale = 1.0 + dot((iota((n_dev, buckets), 1) == times).astype(BF16), bank[conc_dev + buckets :, :])
    one_hot = (iota((n_dev, conc_dev), 1) == mine).astype(BF16)
    offset = mean_1 + dot(one_hot, bank[0:conc_dev, :]) * mean_2
    coef_wait(0)
    factor = jnp.broadcast_to(coef[...], out.shape)
    size = parts // chunks
    grad = jnp.zeros((n_dev, weight.shape[0]), F32)
    for i in range(chunks):
        dkv = jnp.concatenate([piece(r).astype(BF16) for r in range(i * size, (i + 1) * size)], 1)
        wait(i)
        grad += dot_nt(dkv, weight[:, i * size * head_dim : (i + 1) * size * head_dim])
    high, low = split_bf16(grad * scale - offset)
    out[...] = dot(owned, jnp.concatenate([high, low], 0)) * factor


def owner_part(packets, bank, n_core, coef, weight):
    each = (bank.shape[0] - SPARE_ROWS) // n_core
    n_each, rows, head_dim = packets[0].shape
    n_dev = n_each * len(packets)
    (out,) = call(
        functools.partial(owner_body, 3),
        [late_part(bank, (0, each)), late(coef, 1), late(weight, 3)] + [direct(x) for x in packets],
        [((coef.shape[0], weight.shape[0]), F32)],
        [pltpu.VMEM((n_dev * rows, head_dim), F32)],
        vmem=GRANT["owner"],
    )
    return out


def exchange(x, axes):
    return lax.all_to_all(x, axes, 0, 0, tiled=True)


def shards(
    txt_tokens,
    concept_table,
    concept_ids,
    positions,
    timesteps,
    counts,
    mod_table,
    kv_weight,
    kv_bias,
    key_gain,
    img_query,
    img_key,
    img_value,
    out_grad,
):
    sizes = tuple(lax.axis_size(a) for a in EVERYONE)
    n_dp, n_chip, n_core = sizes
    _, tok_len, model_width = txt_tokens.shape
    slice_width = kv_weight.shape[0]
    head_dim = key_gain.shape[0]
    conc_dev = concept_table.shape[0]

    def by_core(x):
        return [x] + [
            lax.ppermute(x, "core", [(i, i ^ s) for i in range(n_core)]) for s in range(1, n_core)
        ]

    packets = pack(concept_ids, timesteps, txt_tokens[0], sizes, slice_width, conc_dev)
    packets = exchange(packets, CLASS)
    weights = by_core(kv_weight)
    bank, rstd = table_part(concept_table, by_core(mod_table), slice_width, n_core)
    terms = project(packets, bank, conc_dev, weights, sizes, head_dim, tok_len)
    terms = exchange(terms, CLASS)
    query, grad = img_query[0], out_grad[0]
    stats = image_part(query, img_key[0], img_value[0], grad, head_dim)
    packets = sample_part(
        concept_ids, positions, timesteps, terms, kv_bias.reshape(-1, head_dim), key_gain[None],
        stats, query, grad, sizes, tok_len, conc_dev, model_width,
    )
    packets = by_core(exchange(packets, CLASS))
    coef = rstd / counts.astype(F32)[:, None]
    return owner_part(packets, bank, n_core, coef, kv_weight)


def solution(mesh):
    n_dp, n_fsdp = mesh.shape["dp"], mesh.shape["fsdp"]
    n_core = 2 if n_fsdp % 2 == 0 else 1
    fine = Mesh(mesh.devices.reshape(n_dp, n_fsdp // n_core, n_core), ("dp", "chip", "core"))
    fsdp = ("chip", "core")
    every = ("dp",) + fsdp
    placed = (
        P(every, None, None),
        P("dp", None),
        P(every),
        P(every),
        P(every),
        P("dp"),
        P(None, None, fsdp),
        P(fsdp, None),
        P(),
        P(),
        P(every, None, None),
        P(every, None, None),
        P(every, None, None),
        P(every, None, None),
    )
    return jax.shard_map(
        shards, mesh=fine, in_specs=placed, out_specs=P("dp", fsdp), check_vma=False
    )
```
